256 devices in a mesh: row: 8 (over x, y_hi), col: 32 (over y_lo, z, core).
Axes of the slice: x: 4, y: 4 (y_hi: 2, y_lo: 2; y = y_hi * 2 + y_lo), z: 8, core: 2. Of those that a mesh axis runs over, the one named last changes fastest.
Arguments:
- jacobian: bfloat16 [1024, 131072], P('row', 'col'), may hold values from -6 to 6
- cov_rows: bfloat16 [512, 131072], P('row', 'col'), may hold values from -6 to 9, as said below
- sens_carry: bfloat16 [1024, 131072], P('row', 'col'), may hold values from -6 to 6
Outputs:
- sensitivity: bfloat16 [1024, 131072], P('row', 'col')
- innovation: float32 [1024, 1024], P('row', 'col')
The draws below stay inside these ranges and needn't reach their ends.
Inputs may be any that keep to these rules, and one draw needn't show every extreme that they name: cov_rows row k holds parameter k's prior cross-terms with every parameter; no symmetry or definiteness of these rows is promised.
All inputs are finite; a program needn't handle non-finite values.
Results may differ from the reference program's by a relative error of at most 0.0031.
Values may be sent and summed in bfloat16 or wider, within the bound.
No kernel may reach another device: no remote copies, remote signals or barrier semaphores. Data moves between devices by JAX's collectives and lax.ppermute only.
A program may use at most 64 MiB of HBM per device.

```python
import math
import jax
import jax.numpy as jnp
from jax import lax

PARAMS = 131072
PANEL = 256
PANELS = 2
TARGETS = 1024


def draw_cov_rows(key, part):
    key = jax.random.fold_in(key, 11)
    width = PANELS * PANEL
    base_key = jax.random.fold_in(key, 0)
    base = jnp.clip(jax.random.normal(base_key, (width, PARAMS), jnp.float32), -6.0, 6.0)
    rows_index = jnp.arange(width)[:, None]
    cols_index = jnp.arange(PARAMS)[None, :]
    diagonal = jnp.where(rows_index == cols_index, 3.0, 0.0).astype(jnp.float32)
    return (base + diagonal).astype(jnp.bfloat16)


def block_scale(own_key, extent, cuts, smallest, high):
    factor_of, own = 1.0, jax.random.fold_in(own_key, 6)
    for position, parts in cuts:
        draws = jnp.exp(jax.random.uniform(jax.random.fold_in(own, position), (parts,), jnp.float32, smallest / len(cuts), high / len(cuts)))
        factor_of = factor_of * jnp.repeat(draws, extent[position] // parts).reshape([-1 if axis == position else 1 for axis in range(len(extent))])
    return factor_of


def normal_values(own_key, dims, scale, limit, cuts=(), kind=jnp.bfloat16):
    result = jax.random.normal(own_key, dims, jnp.float32) * scale
    if len(cuts) > 0:
        result = block_scale(own_key, dims, cuts, -0.22, 0.18) * result
    return jnp.clip(result, min=-limit, max=limit).astype(kind)


def setup_inputs(seed: int = 0) -> dict:
    splits = jax.random.split(jax.random.key(seed), 4)
    return {
        "jacobian": normal_values(splits[0], (TARGETS, PARAMS), 1.0, 6.0, ((0, 8), (1, 32))),
        "cov_rows": draw_cov_rows(jax.random.fold_in(splits[3], 71), 0),
        "sens_carry": normal_values(splits[2], (TARGETS, PARAMS), 1.0, 6.0, ((0, 8), (1, 32))),
    }


def reference(jacobian, cov_rows, sens_carry):
    width = PANELS * PANEL
    span_cols = min(8192, PARAMS)
    blocks = PARAMS // span_cols
    jac_panel = jacobian[:, :width]
    cov_blocks = cov_rows.reshape(width, blocks, span_cols).transpose(1, 0, 2)
    jac_blocks = jacobian.reshape(TARGETS, blocks, span_cols).transpose(1, 0, 2)
    carry_blocks = sens_carry.reshape(TARGETS, blocks, span_cols).transpose(1, 0, 2)
    panel_factor = 1.0 / math.sqrt(width)

    def advance(carry, triple):
        cov_part, jac_part, prior_part = triple
        product = jnp.dot(jac_panel, cov_part, preferred_element_type=jnp.float32) * panel_factor
        sens_part = (prior_part.astype(jnp.float32) + product).astype(jnp.bfloat16)
        carry = carry + jnp.dot(sens_part.astype(jnp.float32), jac_part.astype(jnp.float32).T)
        return (carry, sens_part)
    start_sum = jnp.zeros((TARGETS, TARGETS), jnp.float32)
    summed, pieces = lax.scan(advance, start_sum, (cov_blocks, jac_blocks, carry_blocks))
    sensitivity = pieces.transpose(1, 0, 2).reshape(TARGETS, PARAMS)
    innovation = summed * (1.0 / math.sqrt(PARAMS))
    return (sensitivity, innovation)
```

```python
import math

import jax
import jax.numpy as jnp
from jax import lax
from jax.experimental import pallas as pl
from jax.experimental.pallas import tpu as pltpu
from jax.sharding import Mesh, PartitionSpec as P

PARAMS = 131072
WIDTH = 512
X, H, L, Z, C = 4, 2, 2, 8, 2
AXES = ("x", "h", "l", "z", "c")
ROWS = X * H
SHIFTS = [(dx, dh) for dx in range(X) for dh in range(H)]
ANY = pl.BlockSpec(memory_space=pl.ANY)
VMEM = pl.BlockSpec(memory_space=pltpu.VMEM)
BF16, F32 = jnp.bfloat16, jnp.float32


def pairs(shift, back=False):
    dx, dh = shift
    there = [(x * H + h, ((x + dx) % X) * H + (h ^ dh)) for x in range(X) for h in range(H)]
    return [(b, a) for a, b in there] if back else there


def target(shift):
    dx, dh = shift
    return lax.rem(lax.axis_index("x") + dx, X) * H + lax.rem(lax.axis_index("h") + dh, H)


def source(shift):
    dx, dh = shift
    return lax.rem(lax.axis_index("x") + X - dx, X) * H + lax.rem(lax.axis_index("h") + dh, H)


def call(kernel, outs, ins, out_spec, in_spec, scratch=(), flops=0, nbytes=0):
    return pl.pallas_call(
        kernel,
        out_shape=outs,
        in_specs=[in_spec] * len(ins),
        out_specs=jax.tree.map(lambda _: out_spec, outs),
        scratch_shapes=list(scratch),
        cost_estimate=pl.CostEstimate(flops=flops, bytes_accessed=nbytes, transcendentals=0),
        compiler_params=pltpu.CompilerParams(vmem_limit_bytes=40 * 2**20),
    )(*ins)


def pack_kernel(jac, carry, cov, *rest):
    outs, sems = rest[:ROWS], rest[ROWS]
    copies = []
    for d, shift in enumerate(SHIFTS):
        columns = pl.ds(pl.multiple_of(target(shift) * 512, 512), 512)
        for part, (ref, first, size) in enumerate(((jac, 0, 128), (carry, 128, 128), (cov, 256, 64))):
            copies.append(
                pltpu.make_async_copy(
                    ref.at[:, columns], outs[d].at[pl.ds(first, size), :], sems.at[d * 3 + part]
                )
            )
            copies[-1].start()
    for copy in copies:
        copy.wait()


def split_kernel(*refs):
    pieces, keep, give = refs[:ROWS], refs[ROWS], refs[ROWS + 1]
    core = lax.axis_index("c")
    for d, shift in enumerate(SHIFTS):
        row = source(shift) * 64
        for half in range(2):
            to = pl.ds(pl.multiple_of(row + half * 32, 32), 32)
            mine = pl.ds(pl.multiple_of(half * 64 + core * 32, 32), 32)
            other = pl.ds(pl.multiple_of(half * 64 + (1 - core) * 32, 32), 32)
            keep[to, :] = pieces[d][mine, :]
            give[to, :] = pieces[d][other, :]


def sens_kernel(*refs):
    pieces, panels = refs[:ROWS], refs[ROWS : 2 * ROWS]
    outs, whole, cov = refs[2 * ROWS : 3 * ROWS], refs[3 * ROWS], refs[3 * ROWS + 1]
    for d, shift in enumerate(SHIFTS):
        cov[pl.ds(pl.multiple_of(source(shift) * 64, 64), 64), :] = pieces[d][256:320, :]
    for d in range(ROWS):
        product = jnp.dot(panels[d][...], cov[...], preferred_element_type=F32)
        value = pieces[d][128:256, :].astype(F32) + product * (1.0 / math.sqrt(WIDTH))
        value = value.astype(BF16)
        outs[d][...] = value
        whole[d * 128 : (d + 1) * 128, :] = value


def innov_kernel(keep, got, sens, sens_got, own, *outs):
    dims = (((1,), (1,)), ((), ()))
    for block in range(4):
        rows = pl.ds(block * 128, 128)
        value = lax.dot_general(keep[rows, :], sens[...], dims, preferred_element_type=F32)
        value += lax.dot_general(got[rows, :], sens_got[...], dims, preferred_element_type=F32)
        own[rows, :] = value[:, :128]
        for d in range(1, ROWS):
            outs[d - 1][rows, :] = value[:, d * 128 : (d + 1) * 128].astype(BF16)


def sum_kernel(own, *refs):
    out = refs[-1]
    total = own[...]
    for ref in refs[:-1]:
        total += ref[...].astype(F32)
    out[...] = total.astype(BF16)


def final_kernel(got, out):
    total = got[0].astype(F32)
    for k in range(1, L * Z):
        total += got[k].astype(F32)
    out[...] = total * (1.0 / math.sqrt(PARAMS))


def assemble_kernel(*refs):
    pieces, out, sems = refs[:ROWS], refs[ROWS], refs[ROWS + 1]
    copies = []
    for d, shift in enumerate(SHIFTS):
        columns = pl.ds(pl.multiple_of(target(shift) * 512, 512), 512)
        copies.append(pltpu.make_async_copy(pieces[d], out.at[:, columns], sems.at[d]))
        copies[-1].start()
    for copy in copies:
        copy.wait()


FIRST = [[((0, 0), (0, 4))], [((0, 0), (1, 2))], [((0, 0), (1, 6))]]
SECOND = [
    [((0, 0), (0, 1)), ((0, 4), (0, 3)), ((1, 2), (1, 1)), ((1, 6), (1, 5))],
    [((0, 0), (0, 7)), ((0, 4), (0, 5)), ((1, 2), (1, 3)), ((1, 6), (1, 7))],
    [((0, 0), (1, 0)), ((0, 4), (1, 4)), ((1, 2), (0, 2)), ((1, 6), (0, 6))],
]


def spread_panel(value):
    at = lax.axis_index("l") * Z + lax.axis_index("z")
    for stage in (FIRST, SECOND):
        received = []
        for group in stage:
            perm = [(a[0] * Z + a[1], b[0] * Z + b[1]) for a, b in group]
            hit = jnp.zeros((), jnp.bool_)
            for _, b in perm:
                hit = hit | (at == b)
            received.append((hit, lax.ppermute(value, ("l", "z"), perm)))
        for hit, got in received:
            value = jnp.where(hit, got, value)
    got = lax.ppermute(value, "c", [(0, 1)])
    return jnp.where(lax.axis_index("c") == 1, got, value)


def body(jacobian, cov_rows, sens_carry):
    shape = jax.ShapeDtypeStruct
    panel = spread_panel(jacobian[:, :WIDTH])
    packed = call(
        pack_kernel,
        [shape((320, 512), BF16)] * ROWS,
        (jacobian, sens_carry, cov_rows),
        ANY,
        ANY,
        scratch=[pltpu.SemaphoreType.DMA((3 * ROWS,))],
        nbytes=5 * 2**20,
    )
    pieces = [packed[0]] + [
        lax.ppermute(packed[d], ("x", "h"), pairs(SHIFTS[d])) for d in range(1, ROWS)
    ]
    keep, give = call(
        split_kernel, [shape((512, 512), BF16)] * 2, pieces, VMEM, VMEM, nbytes=4 * 2**20
    )
    got = lax.ppermute(give, "c", [(0, 1), (1, 0)])
    panels = [panel] + [
        lax.ppermute(panel, ("x", "h"), pairs(SHIFTS[d])) for d in range(1, ROWS)
    ]
    *sens, whole = call(
        sens_kernel,
        [shape((128, 512), BF16)] * ROWS + [shape((1024, 512), BF16)],
        (*pieces, *panels),
        VMEM,
        VMEM,
        scratch=[pltpu.VMEM((512, 512), BF16)],
        flops=2 * 1024 * 512 * 512,
        nbytes=6 * 2**20,
    )
    whole_got = lax.ppermute(whole, "c", [(0, 1), (1, 0)])
    own, *parts = call(
        innov_kernel,
        [shape((512, 128), F32)] + [shape((512, 128), BF16)] * (ROWS - 1),
        (keep, got, whole, whole_got),
        VMEM,
        VMEM,
        flops=2 * 512 * 1024 * 1024,
        nbytes=4 * 2**20,
    )
    parts_got = [
        lax.ppermute(parts[d - 1], ("x", "h"), pairs(SHIFTS[d], True)) for d in range(1, ROWS)
    ]
    summed = call(
        sum_kernel, shape((512, 128), BF16), (own, *parts_got), VMEM, VMEM, nbytes=2**20
    )
    sens_got = [sens[0]] + [
        lax.ppermute(sens[d], ("x", "h"), pairs(SHIFTS[d], True)) for d in range(1, ROWS)
    ]
    shared = lax.all_to_all(
        summed.reshape(L * Z, 32, 128), ("l", "z"), split_axis=0, concat_axis=0, tiled=True
    )
    innovation = call(final_kernel, shape((32, 128), F32), (shared,), VMEM, VMEM, nbytes=2**17)
    sensitivity = call(
        assemble_kernel,
        shape((128, 4096), BF16),
        sens_got,
        ANY,
        ANY,
        scratch=[pltpu.SemaphoreType.DMA((ROWS,))],
        nbytes=2 * 2**20,
    )
    return (sensitivity, innovation.T)


def solution(mesh):
    fine = Mesh(mesh.devices.reshape(X, H, L, Z, C), AXES)
    spec = P(("x", "h"), ("l", "z", "c"))
    return jax.shard_map(
        body, mesh=fine, in_specs=(spec,) * 3, out_specs=(spec,) * 2, check_vma=False
    )
```

```python
import math

import jax
import jax.numpy as jnp
from jax import lax
from jax.experimental import pallas as pl
from jax.experimental.pallas import tpu as pltpu
from jax.sharding import Mesh, PartitionSpec as P

PARAMS = 131072
WIDTH = 512
X, H, L, Z, C = 4, 2, 2, 8, 2
AXES = ("x", "h", "l", "z", "c")
ANY = pl.BlockSpec(memory_space=pl.ANY)
VMEM = pl.BlockSpec(memory_space=pltpu.VMEM)
BF16, F32 = jnp.bfloat16, jnp.float32
SWAP = [(0, 1), (1, 0)]
MIB = 2**20


def source(d):
    return lax.rem(lax.axis_index("x") + X - d, X)


def call(kernel, outs, ins, spec, scratch=(), flops=0, nbytes=0, vmem=4):
    return pl.pallas_call(
        kernel,
        out_shape=outs,
        in_specs=[spec] * len(ins),
        out_specs=jax.tree.map(lambda _: spec, outs),
        scratch_shapes=list(scratch),
        cost_estimate=pl.CostEstimate(flops=flops, bytes_accessed=nbytes, transcendentals=0),
        compiler_params=pltpu.CompilerParams(vmem_limit_bytes=vmem * MIB),
    )(*ins)


def shape(*dims, kind=BF16):
    return jax.ShapeDtypeStruct(dims, kind)


def run_copies(copies, sems):
    started = [pltpu.make_async_copy(a, b, sems.at[k]) for k, (a, b) in enumerate(copies)]
    for copy in started:
        copy.start()
    for copy in started:
        copy.wait()


def slab(half, core):
    return pl.ds(pl.multiple_of(half * 64 + core * 32, 32), 32)


def give_kernel(jac, give, sems):
    other = 1 - lax.axis_index("c")
    run_copies(
        [(jac.at[slab(k, other), :], give.at[pl.ds(k * 32, 32), :]) for k in range(2)], sems
    )


def pack_kernel(jac, got, cov, first, own, sems):
    core, x = lax.axis_index("c"), lax.axis_index("x")
    mine = pl.ds(pl.multiple_of(x * 1024, 1024), 1024)
    copies = []
    for k in range(X + 1):
        columns = pl.ds(k * 1024, 1024) if k < X else mine
        to = first.at[k] if k < X else own
        copies += [(jac.at[slab(n, core), columns], to.at[pl.ds(n * 32, 32), :]) for n in range(2)]
        copies.append((got.at[:, columns], to.at[pl.ds(64, 64), :]))
        copies.append((cov.at[:, columns], to.at[pl.ds(128, 64), :]))
    run_copies(copies, sems)


def carry_kernel(carry, out, sems):
    run_copies([(carry.at[:, pl.ds(k * 1024, 1024)], out.at[k]) for k in range(X)], sems)


def rest_kernel(first, own_got, cov, jac, sems):
    copies = []
    for d in range(1, X):
        at = source(d)
        copies.append((first.at[at, pl.ds(128, 64), :], cov.at[d - 1]))
        copies.append((first.at[at, pl.ds(0, 128), :], jac.at[d - 1]))
    run_copies(copies, sems)


def sens_kernel(first, own_got, cov_got, carry, *refs):
    panels, outs, cov = refs[:X], refs[X : 2 * X], refs[2 * X]
    h = lax.axis_index("h")

    def rows(x, side):
        return pl.ds(pl.multiple_of((x * H + side) * 64, 64), 64)

    for k in range(X):
        cov[rows(k, h), :] = first[k, 128:192, :]
    cov[rows(source(0), 1 - h), :] = own_got[128:192, :]
    for d in range(1, X):
        cov[rows(source(d), 1 - h), :] = cov_got[d - 1]
    for d in range(X):
        product = jnp.dot(panels[d][...], cov[...], preferred_element_type=F32)
        value = carry[source(d)].astype(F32) + product * (1.0 / math.sqrt(WIDTH))
        outs[d][...] = value.astype(BF16)


def innov_kernel(first, own_got, jac_got, *refs):
    sens, sens_got, own, parts = refs[:X], refs[X : 2 * X], refs[2 * X], refs[2 * X + 1]
    h, x = lax.axis_index("h"), lax.axis_index("x")
    dims = (((1,), (1,)), ((), ()))
    chunks = [(first.at[k], k * H + h) for k in range(X)]
    chunks.append((own_got, x * H + 1 - h))
    chunks += [(jac_got.at[d - 1], source(d) * H + 1 - h) for d in range(1, X)]
    for ref, row in chunks:
        to = pl.ds(pl.multiple_of(row * 64, 64), 64)
        for d in range(X):
            value = lax.dot_general(ref[0:64, :], sens[d][...], dims, preferred_element_type=F32)
            value += lax.dot_general(
                ref[64:128, :], sens_got[d][...], dims, preferred_element_type=F32
            )
            parts[source(d), to, :] = value.astype(BF16)
            if d == 0:
                own[to, :] = value


def sum_kernel(own, got, out):
    total = own[...]
    x = lax.axis_index("x")
    for k in range(X):
        total += jnp.where(x == k, 0.0, got[k].astype(F32))
    out[...] = total.astype(BF16)


def final_kernel(got, out):
    total = got[0].astype(F32)
    for k in range(1, L * Z):
        total += got[k].astype(F32)
    out[...] = total * (1.0 / math.sqrt(PARAMS))


def assemble_kernel(*refs):
    pieces, out, sems = refs[:X], refs[X], refs[X + 1]
    copies = []
    for d in range(X):
        at = lax.rem(lax.axis_index("x") + d, X)
        copies.append((pieces[d], out.at[:, pl.ds(pl.multiple_of(at * 1024, 1024), 1024)]))
    run_copies(copies, sems)


FIRST = [[((0, 0), (0, 4))], [((0, 0), (1, 2))], [((0, 0), (1, 6))]]
SECOND = [
    [((0, 0), (0, 1)), ((0, 4), (0, 3)), ((1, 2), (1, 1)), ((1, 6), (1, 5))],
    [((0, 0), (0, 7)), ((0, 4), (0, 5)), ((1, 2), (1, 3)), ((1, 6), (1, 7))],
    [((0, 0), (1, 0)), ((0, 4), (1, 4)), ((1, 2), (0, 2)), ((1, 6), (0, 6))],
]


def spread_panel(value):
    at = lax.axis_index("l") * Z + lax.axis_index("z")
    for stage in (FIRST, SECOND):
        received = []
        for group in stage:
            perm = [(a[0] * Z + a[1], b[0] * Z + b[1]) for a, b in group]
            hit = jnp.zeros((), jnp.bool_)
            for _, b in perm:
                hit = hit | (at == b)
            received.append((hit, lax.ppermute(value, ("l", "z"), perm)))
        for hit, got in received:
            value = jnp.where(hit, got, value)
    got = lax.ppermute(value, "c", [(0, 1)])
    return jnp.where(lax.axis_index("c") == 1, got, value)


def ring(d):
    return [(x, (x + d) % X) for x in range(X)]


def over(value, axes):
    return lax.all_to_all(value, axes, split_axis=0, concat_axis=0, tiled=True)


def dma(n):
    return [pltpu.SemaphoreType.DMA((n,))]


def body(jacobian, cov_rows, sens_carry):
    give = call(give_kernel, shape(64, 4096), (jacobian,), ANY, dma(2), nbytes=MIB)
    got = lax.ppermute(give, "c", SWAP)
    packed, own = call(
        pack_kernel,
        [shape(X, 192, 1024), shape(192, 1024)],
        (jacobian, got, cov_rows),
        ANY,
        dma(4 * (X + 1)),
        nbytes=4 * MIB,
    )
    own_got = lax.ppermute(own, "h", SWAP)
    panel = spread_panel(jacobian[:, :WIDTH])
    panels = [panel] + [lax.ppermute(panel, "x", ring(d)) for d in range(1, X)]
    first = over(packed, "x")
    cov_rest, jac_rest = call(
        rest_kernel,
        [shape(X - 1, 64, 1024), shape(X - 1, 128, 1024)],
        (first, own_got),
        ANY,
        dma(2 * X - 2),
        nbytes=2 * MIB,
    )
    cov_got = lax.ppermute(cov_rest, "h", SWAP)
    jac_got = lax.ppermute(jac_rest, "h", SWAP)
    carry = over(
        call(carry_kernel, shape(X, 128, 1024), (sens_carry,), ANY, dma(X), nbytes=2 * MIB), "x"
    )
    sens = call(
        sens_kernel,
        [shape(128, 1024)] * X,
        (first, own_got, cov_got, carry, *panels),
        VMEM,
        [pltpu.VMEM((512, 1024), BF16)],
        flops=2 * 512 * 512 * 1024,
        nbytes=2 * MIB,
        vmem=16,
    )
    sens_got = [lax.ppermute(part, "c", SWAP) for part in sens]
    own_sum, parts = call(
        innov_kernel,
        [shape(512, 128, kind=F32), shape(X, 512, 128)],
        (first, own_got, jac_got, *sens, *sens_got),
        VMEM,
        flops=2 * 512 * 512 * 2048,
        nbytes=2 * MIB,
        vmem=16,
    )
    summed = call(sum_kernel, shape(512, 128), (own_sum, over(parts, "x")), VMEM, nbytes=MIB)
    sens_back = [sens[0]] + [lax.ppermute(sens[d], "x", ring(-d)) for d in range(1, X)]
    shared = over(summed.reshape(L * Z, 32, 128), ("l", "z"))
    innovation = call(final_kernel, shape(32, 128, kind=F32), (shared,), VMEM, nbytes=2**17)
    sensitivity = call(
        assemble_kernel, shape(128, 4096), sens_back, ANY, dma(X), nbytes=2 * MIB
    )
    return (sensitivity, innovation.T)


def solution(mesh):
    fine = Mesh(mesh.devices.reshape(X, H, L, Z, C), AXES)
    spec = P(("x", "h"), ("l", "z", "c"))
    return jax.shard_map(
        body, mesh=fine, in_specs=(spec,) * 3, out_specs=(spec,) * 2, check_vma=False
    )
```

```python
import functools
import math

import jax
import jax.numpy as jnp
from jax import lax
from jax.experimental import pallas as pl
from jax.experimental.pallas import tpu as pltpu
from jax.sharding import Mesh, PartitionSpec as P

PARAMS = 131072
WIDTH = 512
X, H, L, Z, C = 4, 2, 2, 8, 2
AXES = ("x", "h", "l", "z", "c")
ANY = pl.BlockSpec(memory_space=pl.ANY)
VMEM = pl.BlockSpec(memory_space=pltpu.VMEM)
BF16, F32 = jnp.bfloat16, jnp.float32
SWAP = [(0, 1), (1, 0)]
MIB = 2**20


def source(d):
    return lax.rem(lax.axis_index("x") + X - d, X)


def call(kernel, outs, ins, spec, scratch=(), flops=0, nbytes=0, vmem=1, behind=()):
    return pl.pallas_call(
        kernel,
        out_shape=outs,
        in_specs=[spec] * len(ins) + [ANY] * len(behind),
        out_specs=jax.tree.map(lambda _: spec, outs),
        scratch_shapes=list(scratch),
        cost_estimate=pl.CostEstimate(flops=flops, bytes_accessed=nbytes, transcendentals=0),
        compiler_params=pltpu.CompilerParams(vmem_limit_bytes=vmem * MIB),
    )(*ins, *behind)


def shape(*dims, kind=BF16):
    return jax.ShapeDtypeStruct(dims, kind)


def run_copies(copies, sems):
    started = [pltpu.make_async_copy(a, b, sems.at[k]) for k, (a, b) in enumerate(copies)]
    for copy in started:
        copy.start()
    for copy in started:
        copy.wait()


def slab(half, core):
    return pl.ds(pl.multiple_of(half * 64 + core * 32, 32), 32)


def give_kernel(jac, give, sems):
    other = 1 - lax.axis_index("c")
    run_copies(
        [(jac.at[slab(k, other), :], give.at[pl.ds(k * 32, 32), :]) for k in range(2)], sems
    )


def pack_kernel(jac, got, cov, first, own, sems):
    core, x = lax.axis_index("c"), lax.axis_index("x")
    mine = pl.ds(pl.multiple_of(x * 1024, 1024), 1024)
    copies = []
    for k in range(X + 1):
        columns = pl.ds(k * 1024, 1024) if k < X else mine
        to = first.at[k] if k < X else own
        copies += [(jac.at[slab(n, core), columns], to.at[pl.ds(n * 32, 32), :]) for n in range(2)]
        copies.append((got.at[:, columns], to.at[pl.ds(64, 64), :]))
        copies.append((cov.at[:, columns], to.at[pl.ds(128, 64), :]))
    run_copies(copies, sems)


def carry_kernel(carry, panel, out, sems):
    copies = []
    for k in range(X):
        copies.append((carry.at[:, pl.ds(k * 1024, 1024)], out.at[k, pl.ds(0, 128), :]))
        for n in range(2):
            copies.append(
                (
                    panel.at[pl.ds(n * 64, 64), :],
                    out.at[k, pl.ds(128, 64), pl.ds(n * WIDTH, WIDTH)],
                )
            )
    run_copies(copies, sems)


def rest_kernel(first, own_got, cov, jac, sems):
    copies = []
    for d in range(1, X):
        at = source(d)
        copies.append((first.at[at, pl.ds(128, 64), :], cov.at[d - 1]))
        copies.append((first.at[at, pl.ds(0, 128), :], jac.at[d - 1]))
    run_copies(copies, sems)


def sens_kernel(first, own_got, cov_got, second, *refs):
    outs, cov, panel = refs[:X], refs[X], refs[X + 1]
    h = lax.axis_index("h")

    def rows(x, side):
        return pl.ds(pl.multiple_of((x * H + side) * 64, 64), 64)

    for k in range(X):
        cov[rows(k, h), :] = first[k, 128:192, :]
    cov[rows(source(0), 1 - h), :] = own_got[128:192, :]
    for d in range(1, X):
        cov[rows(source(d), 1 - h), :] = cov_got[d - 1]
    for d in range(X):
        at = source(d)
        for n in range(2):
            panel[d * 128 + n * 64 : d * 128 + n * 64 + 64, :] = second[
                at, 128:192, n * WIDTH : (n + 1) * WIDTH
            ]
    for d in range(X):
        rows = slice(d * 128, (d + 1) * 128)
        product = jnp.dot(panel[rows, :], cov[...], preferred_element_type=F32)
        value = second[source(d), 0:128, :].astype(F32) + product * (1.0 / math.sqrt(WIDTH))
        outs[d][...] = value.astype(BF16)


def innov_kernel(first, own_got, jac_got, *refs):
    sens, sens_got, (own, parts, jac, both) = refs[:X], refs[X : 2 * X], refs[-4:]
    h, x = lax.axis_index("h"), lax.axis_index("x")
    chunks = [(first.at[k], k * H + h) for k in range(X)]
    chunks.append((own_got, x * H + 1 - h))
    chunks += [(jac_got.at[d - 1], source(d) * H + 1 - h) for d in range(1, X)]
    for ref, row in chunks:
        to = pl.ds(pl.multiple_of(row * 64, 64), 64)
        jac[to, 0:1024] = ref[0:64, :]
        jac[to, 1024:2048] = ref[64:128, :]
    for d in range(X):
        both[d * 128 : (d + 1) * 128, 0:1024] = sens[d][...]
        both[d * 128 : (d + 1) * 128, 1024:2048] = sens_got[d][...]
    for block in range(4):
        to = slice(block * 128, (block + 1) * 128)
        value = lax.dot_general(
            jac[to, :], both[...], (((1,), (1,)), ((), ())), preferred_element_type=F32
        )
        own[to, :] = value[:, 0:128]
        for d in range(X):
            parts[source(d), to, :] = value[:, d * 128 : (d + 1) * 128].astype(BF16)


def sum_kernel(own, got, out):
    total = own[...]
    x = lax.axis_index("x")
    for k in range(X):
        total += jnp.where(x == k, 0.0, got[k].astype(F32))
    out[...] = total.astype(BF16)


def final_kernel(got, out):
    total = got[0].astype(F32)
    for k in range(1, L * Z):
        total += got[k].astype(F32)
    out[...] = total * (1.0 / math.sqrt(PARAMS))


def assemble_kernel(*refs):
    pieces, out, sems = refs[:X], refs[X], refs[X + 1]
    copies = []
    for d in range(X):
        at = lax.rem(lax.axis_index("x") + d, X)
        copies.append((pieces[d], out.at[:, pl.ds(pl.multiple_of(at * 1024, 1024), 1024)]))
    run_copies(copies, sems)


FIRST = [[((0, 0), (0, 4))], [((0, 0), (1, 2))], [((0, 0), (1, 6))]]
SECOND = [
    [((0, 0), (0, 1)), ((0, 4), (0, 3)), ((1, 2), (1, 1)), ((1, 6), (1, 5))],
    [((0, 0), (0, 7)), ((0, 4), (0, 5)), ((1, 2), (1, 3)), ((1, 6), (1, 7))],
    [((0, 0), (1, 0)), ((0, 4), (1, 4)), ((1, 2), (0, 2)), ((1, 6), (0, 6))],
]


def choose_kernel(groups, value, *refs):
    received, out = refs[: len(groups)], refs[-1]
    at = lax.axis_index("l") * Z + lax.axis_index("z")
    out[...] = value[...]
    for perm, ref in zip(groups, received):
        hit = at == perm[0][1]
        for _, b in perm[1:]:
            hit = hit | (at == b)

        @pl.when(hit)
        def _():
            out[...] = ref[...]


def core_kernel(value, got, out):
    core = lax.axis_index("c")

    @pl.when(core == 0)
    def _():
        out[...] = value[...]

    @pl.when(core == 1)
    def _():
        out[...] = got[...]


def panel_call(kernel, ins, behind=()):
    return pl.pallas_call(
        kernel,
        out_shape=shape(128, WIDTH),
        in_specs=[VMEM] * len(ins) + [ANY] * len(behind),
        out_specs=VMEM,
        cost_estimate=pl.CostEstimate(flops=0, bytes_accessed=2**18, transcendentals=0),
        compiler_params=pltpu.CompilerParams(vmem_limit_bytes=2 * MIB),
    )(*ins, *behind)


def spread_panel(value, behind):
    for number, stage in enumerate((FIRST, SECOND)):
        groups = [[(a[0] * Z + a[1], b[0] * Z + b[1]) for a, b in group] for group in stage]
        received = [lax.ppermute(value, ("l", "z"), perm) for perm in groups]
        value = panel_call(
            functools.partial(choose_kernel, groups), (value, *received), behind if number else ()
        )
    return panel_call(core_kernel, (value, lax.ppermute(value, "c", [(0, 1)])))


def ring(d):
    return [(x, (x + d) % X) for x in range(X)]


def over(value, axes):
    return lax.all_to_all(value, axes, split_axis=0, concat_axis=0, tiled=True)


def dma(n):
    return [pltpu.SemaphoreType.DMA((n,))]


def body(jacobian, cov_rows, sens_carry):
    give = call(give_kernel, shape(64, 4096), (jacobian,), ANY, dma(2), nbytes=MIB)
    got = lax.ppermute(give, "c", SWAP)
    packed, own = call(
        pack_kernel,
        [shape(X, 192, 1024), shape(192, 1024)],
        (jacobian, got, cov_rows),
        ANY,
        dma(4 * (X + 1)),
        nbytes=4 * MIB,
    )
    own_got = lax.ppermute(own, "h", SWAP)
    panel = spread_panel(jacobian[:, :WIDTH], (own_got,))
    first = over(packed, "x")
    cov_rest, jac_rest = call(
        rest_kernel,
        [shape(X - 1, 64, 1024), shape(X - 1, 128, 1024)],
        (first, own_got),
        ANY,
        dma(2 * X - 2),
        nbytes=2 * MIB,
    )
    cov_got = lax.ppermute(cov_rest, "h", SWAP)
    jac_got = lax.ppermute(jac_rest, "h", SWAP)
    packed = call(
        carry_kernel, shape(X, 192, 1024), (sens_carry, panel), ANY, dma(3 * X), nbytes=2 * MIB
    )
    second = over(packed, "x")
    sens = call(
        sens_kernel,
        [shape(128, 1024)] * X,
        (first, own_got, cov_got, second),
        VMEM,
        [pltpu.VMEM((512, 1024), BF16), pltpu.VMEM((512, WIDTH), BF16)],
        flops=2 * 512 * 512 * 1024,
        nbytes=2 * MIB,
        vmem=12,
    )
    sens_back = [sens[0]] + [lax.ppermute(sens[d], "x", ring(-d)) for d in range(1, X)]
    sens_got = [lax.ppermute(part, "c", SWAP) for part in sens]
    own_sum, parts = call(
        innov_kernel,
        [shape(512, 128, kind=F32), shape(X, 512, 128)],
        (first, own_got, jac_got, *sens, *sens_got),
        VMEM,
        [pltpu.VMEM((512, 2048), BF16)] * 2,
        flops=2 * 512 * 512 * 2048,
        nbytes=2 * MIB,
        vmem=16,
        behind=(sens_back[1], sens_back[3]),
    )
    summed = call(sum_kernel, shape(512, 128), (own_sum, over(parts, "x")), VMEM, nbytes=MIB, vmem=4)
    shared = over(summed.reshape(L * Z, 32, 128), ("l", "z"))
    innovation = call(final_kernel, shape(32, 128, kind=F32), (shared,), VMEM, nbytes=2**17, vmem=4)
    sensitivity = call(
        assemble_kernel, shape(128, 4096), sens_back, ANY, dma(X), nbytes=2 * MIB
    )
    return (sensitivity, innovation.T)


def solution(mesh):
    fine = Mesh(mesh.devices.reshape(X, H, L, Z, C), AXES)
    spec = P(("x", "h"), ("l", "z", "c"))
    return jax.shard_map(
        body, mesh=fine, in_specs=(spec,) * 3, out_specs=(spec,) * 2, check_vma=False
    )
```

```python
import math

import jax
import jax.numpy as jnp
from jax import lax
from jax.experimental import pallas as pl
from jax.experimental.pallas import tpu as pltpu
from jax.sharding import Mesh, PartitionSpec as P

PARAMS = 131072
WIDTH = 512
X, H, L, Z, C = 4, 2, 2, 8, 2
AXES = ("x", "h", "l", "z", "c")
ANY = pl.BlockSpec(memory_space=pl.ANY)
VMEM = pl.BlockSpec(memory_space=pltpu.VMEM)
BF16, F32 = jnp.bfloat16, jnp.float32
SWAP = [(0, 1), (1, 0)]
MIB = 2**20


def source(d):
    return lax.rem(lax.axis_index("x") + X - d, X)


def call(kernel, outs, ins, spec, scratch=(), flops=0, nbytes=0, vmem=1, behind=()):
    return pl.pallas_call(
        kernel,
        out_shape=outs,
        in_specs=[spec] * len(ins) + [ANY] * len(behind),
        out_specs=jax.tree.map(lambda _: spec, outs),
        scratch_shapes=list(scratch),
        cost_estimate=pl.CostEstimate(flops=flops, bytes_accessed=nbytes, transcendentals=0),
        compiler_params=pltpu.CompilerParams(vmem_limit_bytes=vmem * MIB),
    )(*ins, *behind)


def shape(*dims, kind=BF16):
    return jax.ShapeDtypeStruct(dims, kind)


def run_copies(copies, sems):
    started = [pltpu.make_async_copy(a, b, sems.at[k]) for k, (a, b) in enumerate(copies)]
    for copy in started:
        copy.start()
    for copy in started:
        copy.wait()


def slab(half, core):
    return pl.ds(pl.multiple_of(half * 64 + core * 32, 32), 32)


def give_kernel(jac, give, sems):
    other = 1 - lax.axis_index("c")
    run_copies(
        [(jac.at[slab(k, other), :], give.at[pl.ds(k * 32, 32), :]) for k in range(2)], sems
    )


def part(d):
    at = lax.rem(lax.axis_index("x") + d, X)
    return pl.ds(pl.multiple_of(at * 1024, 1024), 1024)


def pack_kernel(jac, got, cov, *refs):
    outs, panel, sems, panel_sems = refs[:X], refs[X], refs[X + 1], refs[X + 2]
    core = lax.axis_index("c")

    def pieces(ref, rows):
        return [
            pltpu.make_async_copy(
                ref.at[rows(k), pl.ds(n * 128, 128)], panel.at[k * 4 + n], panel_sems.at[k * 4 + n]
            )
            for k in range(4)
            for n in range(4)
        ]

    @pl.when(core == 0)
    def _():
        for copy in pieces(jac, lambda k: pl.ds(k // 2 * 64 + k % 2 * 16, 16)):
            copy.start()

    @pl.when(core == 1)
    def _():
        for copy in pieces(got, lambda k: pl.ds(k * 16, 16)):
            copy.start()

    copies = []
    for d in range(X):
        copies += [(jac.at[slab(n, core), part(d)], outs[d].at[pl.ds(n * 32, 32), :]) for n in range(2)]
        copies.append((got.at[:, part(d)], outs[d].at[pl.ds(64, 64), :]))
        copies.append((cov.at[:, part(d)], outs[d].at[pl.ds(128, 64), :]))
    run_copies(copies, sems)
    for copy in pieces(got, lambda k: pl.ds(k * 16, 16)):
        copy.wait()


def carry_kernel(carry, *refs):
    run_copies([(carry.at[:, part(d)], refs[d]) for d in range(X)], refs[X])


def rest_kernel(*refs):
    first, cov, jac, sems = refs[: X - 1], refs[-3], refs[-2], refs[-1]
    copies = []
    for d in range(1, X):
        copies.append((first[d - 1].at[pl.ds(128, 64), :], cov.at[d - 1]))
        copies.append((first[d - 1].at[pl.ds(0, 128), :], jac.at[d - 1]))
    run_copies(copies, sems)


def sens_kernel(*refs):
    first, carry, panels, (own_got, cov_got) = refs[:4], refs[4:8], refs[8:12], refs[12:14]
    outs, cov, panel = refs[14:18], refs[18], refs[19]
    h = lax.axis_index("h")

    def rows(d, side):
        return pl.ds(pl.multiple_of((source(d) * H + side) * 64, 64), 64)

    for d in range(X):
        cov[rows(d, h), :] = first[d][128:192, :]
        cov[rows(d, 1 - h), :] = cov_got[d - 1] if d else own_got[128:192, :]
    for d in range(X):
        for k in range(4):
            for n in range(4):
                for core in range(C):
                    at = d * 128 + k // 2 * 64 + core * 32 + k % 2 * 16
                    panel[at : at + 16, n * 128 : n * 128 + 128] = panels[d][(k * 4 + n) * C + core]
    for d in range(X):
        product = jnp.dot(
            panel[d * 128 : (d + 1) * 128, :], cov[...], preferred_element_type=F32
        )
        value = carry[d][...].astype(F32) + product * (1.0 / math.sqrt(WIDTH))
        outs[d][...] = value.astype(BF16)


def innov_kernel(own_got, jac_got, *refs):
    first, sens, sens_got = refs[:X], refs[X : 2 * X], refs[2 * X : 3 * X]
    own, parts, jac, both = refs[-4:]
    h = lax.axis_index("h")
    for d in range(X):
        for side, ref in ((h, first[d]), (1 - h, jac_got.at[d - 1] if d else own_got)):
            to = pl.ds(pl.multiple_of((source(d) * H + side) * 64, 64), 64)
            jac[to, 0:1024] = ref[0:64, :]
            jac[to, 1024:2048] = ref[64:128, :]
        both[d * 128 : (d + 1) * 128, 0:1024] = sens[d][...]
        both[d * 128 : (d + 1) * 128, 1024:2048] = sens_got[d][...]
    value = lax.dot_general(
        jac[...], both[...], (((1,), (1,)), ((), ())), preferred_element_type=F32
    )
    own[...] = value[:, 0:128]
    for d in range(X):
        parts[source(d)] = value[:, d * 128 : (d + 1) * 128].astype(BF16)


def sum_kernel(own, got, out):
    total = own[...]
    x = lax.axis_index("x")
    for k in range(X):
        total += jnp.where(x == k, 0.0, got[k].astype(F32))
    out[...] = total.astype(BF16)


def final_kernel(got, out):
    total = got[0].astype(F32)
    for k in range(1, L * Z):
        total += got[k].astype(F32)
    out[...] = total * (1.0 / math.sqrt(PARAMS))


def assemble_kernel(*refs):
    pieces, out, sems = refs[:X], refs[X], refs[X + 1]
    copies = []
    for d in range(X):
        at = lax.rem(lax.axis_index("x") + d, X)
        copies.append((pieces[d], out.at[:, pl.ds(pl.multiple_of(at * 1024, 1024), 1024)]))
    run_copies(copies, sems)


def ring(d):
    return [(x, (x + d) % X) for x in range(X)]


def over(value, axes):
    return lax.all_to_all(value, axes, split_axis=0, concat_axis=0, tiled=True)


def dma(n):
    return [pltpu.SemaphoreType.DMA((n,))]


def body(jacobian, cov_rows, sens_carry):
    give = call(give_kernel, shape(64, 4096), (jacobian,), ANY, dma(2), nbytes=MIB)
    got = lax.ppermute(give, "c", SWAP)
    *packed, panel = call(
        pack_kernel,
        [shape(192, 1024)] * X + [shape(16, 16, 128)],
        (jacobian, got, cov_rows),
        ANY,
        dma(4 * X) + dma(16),
        nbytes=4 * MIB,
    )
    own_got = lax.ppermute(packed[0], "h", SWAP)
    first = [packed[0]] + [lax.ppermute(packed[d], "x", ring(d)) for d in range(1, X)]
    cov_rest, jac_rest = call(
        rest_kernel,
        [shape(X - 1, 64, 1024), shape(X - 1, 128, 1024)],
        first[1:],
        ANY,
        dma(2 * X - 2),
        nbytes=2 * MIB,
        behind=(own_got,),
    )
    cov_got = lax.ppermute(cov_rest, "h", SWAP)
    jac_got = lax.ppermute(jac_rest, "h", SWAP)
    mine = over(panel, ("l", "z"))[0]
    panel = over(jnp.broadcast_to(mine, (32, 16, 128)), ("l", "z", "c"))
    panels = [panel] + [lax.ppermute(panel, "x", ring(d)) for d in range(1, X)]
    packed = call(
        carry_kernel, [shape(128, 1024)] * X, (sens_carry,), ANY, dma(X), nbytes=2 * MIB
    )
    carry = [packed[0]] + [lax.ppermute(packed[d], "x", ring(d)) for d in range(1, X)]
    sens = call(
        sens_kernel,
        [shape(128, 1024)] * X,
        (*first, *carry, *panels, own_got, cov_got),
        VMEM,
        [pltpu.VMEM((512, 1024), BF16), pltpu.VMEM((512, WIDTH), BF16)],
        flops=2 * 512 * 512 * 1024,
        nbytes=2 * MIB,
        vmem=12,
    )
    sens_back = [sens[0]] + [lax.ppermute(sens[d], "x", ring(-d)) for d in range(1, X)]
    sens_got = [lax.ppermute(part, "c", SWAP) for part in sens]
    own_sum, parts = call(
        innov_kernel,
        [shape(512, 128, kind=F32), shape(X, 512, 128)],
        (own_got, jac_got, *first, *sens, *sens_got),
        VMEM,
        [pltpu.VMEM((512, 2048), BF16)] * 2,
        flops=2 * 512 * 512 * 2048,
        nbytes=2 * MIB,
        vmem=16,
        behind=(sens_back[1], sens_back[3]),
    )
    summed = call(sum_kernel, shape(512, 128), (own_sum, over(parts, "x")), VMEM, nbytes=MIB, vmem=4)
    shared = over(summed.reshape(L * Z, 32, 128), ("l", "z"))
    innovation = call(final_kernel, shape(32, 128, kind=F32), (shared,), VMEM, nbytes=2**17, vmem=4)
    sensitivity = call(
        assemble_kernel, shape(128, 4096), sens_back, ANY, dma(X), nbytes=2 * MIB
    )
    return (sensitivity, innovation.T)


def solution(mesh):
    fine = Mesh(mesh.devices.reshape(X, H, L, Z, C), AXES)
    spec = P(("x", "h"), ("l", "z", "c"))
    return jax.shard_map(
        body, mesh=fine, in_specs=(spec,) * 3, out_specs=(spec,) * 2, check_vma=False
    )
```

```python
import math

import jax
import jax.numpy as jnp
from jax import lax
from jax.experimental import pallas as pl
from jax.experimental.pallas import tpu as pltpu
from jax.sharding import Mesh, PartitionSpec as P

PARAMS = 131072
WIDTH = 512
X, H, L, Z, C = 4, 2, 2, 8, 2
AXES = ("x", "h", "l", "z", "c")
ANY = pl.BlockSpec(memory_space=pl.ANY)
VMEM = pl.BlockSpec(memory_space=pltpu.VMEM)
BF16, F32 = jnp.bfloat16, jnp.float32
SWAP = [(0, 1), (1, 0)]
MIB = 2**20


def source(d):
    return lax.rem(lax.axis_index("x") + X - d, X)


def call(kernel, outs, ins, spec, scratch=(), flops=0, nbytes=0, vmem=1, behind=()):
    return pl.pallas_call(
        kernel,
        out_shape=outs,
        in_specs=[spec] * len(ins) + [ANY] * len(behind),
        out_specs=jax.tree.map(lambda _: spec, outs),
        scratch_shapes=list(scratch),
        cost_estimate=pl.CostEstimate(flops=flops, bytes_accessed=nbytes, transcendentals=0),
        compiler_params=pltpu.CompilerParams(vmem_limit_bytes=vmem * MIB),
    )(*ins, *behind)


def shape(*dims, kind=BF16):
    return jax.ShapeDtypeStruct(dims, kind)


def run_copies(copies, sems):
    started = [pltpu.make_async_copy(a, b, sems.at[k]) for k, (a, b) in enumerate(copies)]
    for copy in started:
        copy.start()
    for copy in started:
        copy.wait()


def slab(half, core):
    return pl.ds(pl.multiple_of(half * 64 + core * 32, 32), 32)


def give_kernel(jac, give, sems):
    other = 1 - lax.axis_index("c")
    run_copies(
        [(jac.at[slab(k, other), :], give.at[pl.ds(k * 32, 32), :]) for k in range(2)], sems
    )


def part(d):
    at = lax.rem(lax.axis_index("x") + d, X)
    return pl.ds(pl.multiple_of(at * 1024, 1024), 1024)


def pack_kernel(jac, got, cov, *refs):
    outs, panel, sems, panel_sems = refs[:X], refs[X], refs[X + 1], refs[X + 2]
    core = lax.axis_index("c")

    def halves(ref, step):
        return [
            pltpu.make_async_copy(
                ref.at[pl.ds(n * step, 32), pl.ds(0, WIDTH)],
                panel.at[pl.ds(n * 32, 32), :],
                panel_sems.at[n],
            )
            for n in range(2)
        ]

    @pl.when(core == 0)
    def _():
        for copy in halves(jac, 64):
            copy.start()

    @pl.when(core == 1)
    def _():
        for copy in halves(got, 32):
            copy.start()

    copies = []
    for d in range(X):
        copies += [(jac.at[slab(n, core), part(d)], outs[d].at[pl.ds(n * 32, 32), :]) for n in range(2)]
        copies.append((got.at[:, part(d)], outs[d].at[pl.ds(64, 64), :]))
        copies.append((cov.at[:, part(d)], outs[d].at[pl.ds(128, 64), :]))
    run_copies(copies, sems)
    for copy in halves(got, 32):
        copy.wait()


def merge_kernel(mine, swapped, near, cross, out):
    core = lax.axis_index("c")
    for here, own, other in ((0, mine, swapped), (1, near, cross)):

        @pl.when(lax.axis_index("l") == here)
        def _():
            for n in range(2):
                out[slab(n, core), :] = own[n * 32 : n * 32 + 32, :]
                out[slab(n, 1 - core), :] = other[n * 32 : n * 32 + 32, :]


def carry_kernel(carry, *refs):
    out, sems = refs[-2:]
    run_copies([(carry.at[:, pl.ds(k * 1024, 1024)], out.at[k]) for k in range(X)], sems)


def rest_kernel(*refs):
    first, cov, jac, sems = refs[: X - 1], refs[-3], refs[-2], refs[-1]
    copies = []
    for d in range(1, X):
        copies.append((first[d - 1].at[pl.ds(128, 64), :], cov.at[d - 1]))
        copies.append((first[d - 1].at[pl.ds(0, 128), :], jac.at[d - 1]))
    run_copies(copies, sems)


def sens_kernel(*refs):
    first, panels, (carry, own_got, cov_got) = refs[:4], refs[4:8], refs[8:11]
    outs, pairs, cov = refs[11:15], refs[15:17], refs[17]
    h = lax.axis_index("h")

    def rows(d, side):
        return pl.ds(pl.multiple_of((source(d) * H + side) * 64, 64), 64)

    for d in range(X):
        cov[rows(d, h), :] = first[d][128:192, :]
        cov[rows(d, 1 - h), :] = cov_got[d - 1] if d else own_got[128:192, :]
    for d in range(X):
        product = jnp.dot(panels[d][...], cov[...], preferred_element_type=F32)
        value = carry[source(d)].astype(F32) + product * (1.0 / math.sqrt(WIDTH))
        value = value.astype(BF16)
        outs[d][...] = value
        pairs[d // 2][d % 2 * 128 : d % 2 * 128 + 128, :] = value


def innov_kernel(own_got, jac_got, *refs):
    first, sens, sens_got = refs[:X], refs[X : X + 2], refs[X + 2 : X + 4]
    parts, jac, both = refs[-3:]
    h = lax.axis_index("h")
    for d in range(X):
        for side, ref in ((h, first[d]), (1 - h, jac_got.at[d - 1] if d else own_got)):
            to = pl.ds(pl.multiple_of((source(d) * H + side) * 64, 64), 64)
            jac[to, 0:1024] = ref[0:64, :]
            jac[to, 1024:2048] = ref[64:128, :]
    for k in range(2):
        both[k * 256 : (k + 1) * 256, 0:1024] = sens[k][...]
        both[k * 256 : (k + 1) * 256, 1024:2048] = sens_got[k][...]
    value = lax.dot_general(
        jac[...], both[...], (((1,), (1,)), ((), ())), preferred_element_type=F32
    )
    for d in range(X):
        parts[source(d)] = value[:, d * 128 : (d + 1) * 128].astype(BF16)


def final_kernel(got, out):
    total = got[0].astype(F32)
    for k in range(1, X * L * Z):
        total += got[k].astype(F32)
    out[...] = total * (1.0 / math.sqrt(PARAMS))


def assemble_kernel(*refs):
    pieces, out, sems = refs[:X], refs[X], refs[X + 1]
    copies = []
    for d in range(X):
        at = lax.rem(lax.axis_index("x") + d, X)
        copies.append((pieces[d], out.at[:, pl.ds(pl.multiple_of(at * 1024, 1024), 1024)]))
    run_copies(copies, sems)


def ring(d):
    return [(x, (x + d) % X) for x in range(X)]


def over(value, axes):
    return lax.all_to_all(value, axes, split_axis=0, concat_axis=0, tiled=True)


def dma(n):
    return [pltpu.SemaphoreType.DMA((n,))]


def body(jacobian, cov_rows, sens_carry):
    give = call(give_kernel, shape(64, 4096), (jacobian,), ANY, dma(2), nbytes=MIB)
    got = lax.ppermute(give, "c", SWAP)
    *packed, panel = call(
        pack_kernel,
        [shape(192, 1024)] * X + [shape(64, WIDTH)],
        (jacobian, got, cov_rows),
        ANY,
        dma(4 * X) + dma(2),
        nbytes=4 * MIB,
    )
    own_got = lax.ppermute(packed[0], "h", SWAP)
    first = [packed[0]] + [lax.ppermute(packed[d], "x", ring(d)) for d in range(1, X)]
    cov_rest, jac_rest = call(
        rest_kernel,
        [shape(X - 1, 64, 1024), shape(X - 1, 128, 1024)],
        first[1:],
        ANY,
        dma(2 * X - 2),
        nbytes=2 * MIB,
        behind=(own_got,),
    )
    cov_got = lax.ppermute(cov_rest, "h", SWAP)
    jac_got = lax.ppermute(jac_rest, "h", SWAP)
    mine = over(jnp.broadcast_to(panel, (Z, 64, WIDTH)), "z")[0]
    swapped = lax.ppermute(mine, ("l", "c"), [(0, 1), (1, 0)])
    near = lax.ppermute(mine, ("l", "c"), [(0, 2), (1, 3)])
    cross = lax.ppermute(mine, ("l", "c"), [(0, 3), (1, 2)])
    panel = call(
        merge_kernel, shape(128, WIDTH), (mine, swapped, near, cross), VMEM, nbytes=2**18
    )
    panels = [panel] + [lax.ppermute(panel, "x", ring(d)) for d in range(1, X)]
    packed = call(
        carry_kernel,
        shape(X, 128, 1024),
        (sens_carry,),
        ANY,
        dma(X),
        nbytes=2 * MIB,
        behind=(mine,),
    )
    carry = over(packed, "x")
    *sens, low, high = call(
        sens_kernel,
        [shape(128, 1024)] * X + [shape(256, 1024)] * 2,
        (*first, *panels, carry, own_got, cov_got),
        VMEM,
        [pltpu.VMEM((512, 1024), BF16)],
        flops=2 * 512 * 512 * 1024,
        nbytes=2 * MIB,
        vmem=12,
    )
    sens_back = [sens[0]] + [lax.ppermute(sens[d], "x", ring(-d)) for d in range(1, X)]
    sens_got = [lax.ppermute(pair, "c", SWAP) for pair in (low, high)]
    parts = call(
        innov_kernel,
        shape(X, 512, 128),
        (own_got, jac_got, *first, low, high, *sens_got),
        VMEM,
        [pltpu.VMEM((512, 2048), BF16)] * 2,
        flops=2 * 512 * 512 * 2048,
        nbytes=2 * MIB,
        vmem=16,
        behind=(sens_back[1], sens_back[3]),
    )
    shared = over(parts.reshape(X * L * Z, 32, 128), ("x", "l", "z"))
    innovation = call(final_kernel, shape(32, 128, kind=F32), (shared,), VMEM, nbytes=2**19, vmem=4)
    sensitivity = call(
        assemble_kernel, shape(128, 4096), sens_back, ANY, dma(X), nbytes=2 * MIB
    )
    return (sensitivity, innovation.T)


def solution(mesh):
    fine = Mesh(mesh.devices.reshape(X, H, L, Z, C), AXES)
    spec = P(("x", "h"), ("l", "z", "c"))
    return jax.shard_map(
        body, mesh=fine, in_specs=(spec,) * 3, out_specs=(spec,) * 2, check_vma=False
    )
```

```python
import functools
import math

import jax
import jax.numpy as jnp
from jax import lax
from jax.experimental import pallas as pl
from jax.experimental.pallas import tpu as pltpu
from jax.sharding import Mesh, PartitionSpec as P

PARAMS = 131072
WIDTH = 512
X, H, L, Z, C = 4, 2, 2, 8, 2
AXES = ("x", "h", "l", "z", "c")
ANY = pl.BlockSpec(memory_space=pl.ANY)
VMEM = pl.BlockSpec(memory_space=pltpu.VMEM)
BF16, F32 = jnp.bfloat16, jnp.float32
SWAP = [(0, 1), (1, 0)]
MIB = 2**20


def source(d):
    return lax.rem(lax.axis_index("x") + X - d, X)


def call(kernel, outs, ins, spec, scratch=(), flops=0, nbytes=0, vmem=1, behind=()):
    return pl.pallas_call(
        kernel,
        out_shape=outs,
        in_specs=[spec] * len(ins) + [ANY] * len(behind),
        out_specs=jax.tree.map(lambda _: spec, outs),
        scratch_shapes=list(scratch),
        cost_estimate=pl.CostEstimate(flops=flops, bytes_accessed=nbytes, transcendentals=0),
        compiler_params=pltpu.CompilerParams(vmem_limit_bytes=vmem * MIB),
    )(*ins, *behind)


def shape(*dims, kind=BF16):
    return jax.ShapeDtypeStruct(dims, kind)


def run_copies(copies, sems):
    started = [pltpu.make_async_copy(a, b, sems.at[k]) for k, (a, b) in enumerate(copies)]
    for copy in started:
        copy.start()
    for copy in started:
        copy.wait()


def slab(half, core):
    return pl.ds(pl.multiple_of(half * 64 + core * 32, 32), 32)


def give_kernel(jac, give, sems):
    other = 1 - lax.axis_index("c")
    run_copies(
        [(jac.at[slab(k, other), :], give.at[pl.ds(k * 32, 32), :]) for k in range(2)], sems
    )


def part(d):
    at = lax.rem(lax.axis_index("x") + d, X)
    return pl.ds(pl.multiple_of(at * 1024, 1024), 1024)


def pack_kernel(jac, got, cov, *refs):
    outs, panel, sems, panel_sems = refs[:X], refs[X], refs[X + 1], refs[X + 2]
    core = lax.axis_index("c")

    def pieces(ref, rows):
        return [
            pltpu.make_async_copy(
                ref.at[rows(k), pl.ds(n * 128, 128)], panel.at[k * 4 + n], panel_sems.at[k * 4 + n]
            )
            for k in range(4)
            for n in range(4)
        ]

    @pl.when(core == 0)
    def _():
        for copy in pieces(jac, lambda k: pl.ds(k // 2 * 64 + k % 2 * 16, 16)):
            copy.start()

    @pl.when(core == 1)
    def _():
        for copy in pieces(got, lambda k: pl.ds(k * 16, 16)):
            copy.start()

    copies = []
    for d in range(X):
        copies += [(jac.at[slab(n, core), part(d)], outs[d].at[pl.ds(n * 32, 32), :]) for n in range(2)]
        copies.append((got.at[:, part(d)], outs[d].at[pl.ds(64, 64), :]))
        copies.append((cov.at[:, part(d)], outs[d].at[pl.ds(128, 64), :]))
    run_copies(copies, sems)
    for copy in pieces(got, lambda k: pl.ds(k * 16, 16)):
        copy.wait()


def carry_kernel(carry, *refs):
    run_copies([(carry.at[:, part(d)], refs[d]) for d in range(X)], refs[X])


def join_kernel(first_row, rows, *refs):
    pieces, out, sems = refs[: X - 1], refs[-2], refs[-1]
    run_copies(
        [(pieces[d].at[pl.ds(first_row, rows), :], out.at[d]) for d in range(X - 1)], sems
    )


def sens_kernel(*refs):
    first, carry, panels, (own_got, cov_got) = refs[:4], refs[4:8], refs[8:12], refs[12:14]
    outs, pairs, cov, panel = refs[14:18], refs[18:20], refs[20], refs[21]
    h = lax.axis_index("h")

    def rows(d, side):
        return pl.ds(pl.multiple_of((source(d) * H + side) * 64, 64), 64)

    for d in range(X):
        cov[rows(d, h), :] = first[d][128:192, :]
        cov[rows(d, 1 - h), :] = cov_got[d - 1] if d else own_got[128:192, :]
    for d in range(X):
        for k in range(4):
            for n in range(4):
                for core in range(C):
                    at = d * 128 + k // 2 * 64 + core * 32 + k % 2 * 16
                    panel[at : at + 16, n * 128 : n * 128 + 128] = panels[d][(k * 4 + n) * C + core]
    for d in range(X):
        product = jnp.dot(
            panel[d * 128 : (d + 1) * 128, :], cov[...], preferred_element_type=F32
        )
        value = carry[d][...].astype(F32) + product * (1.0 / math.sqrt(WIDTH))
        value = value.astype(BF16)
        outs[d][...] = value
        pairs[d // 2][d % 2 * 128 : d % 2 * 128 + 128, :] = value


def innov_kernel(own_got, jac_got, *refs):
    first, sens, sens_got = refs[:X], refs[X : X + 2], refs[X + 2 : X + 4]
    parts, jac, both = refs[-3:]
    h = lax.axis_index("h")
    for d in range(X):
        for side, ref in ((h, first[d]), (1 - h, jac_got.at[d - 1] if d else own_got)):
            to = pl.ds(pl.multiple_of((source(d) * H + side) * 64, 64), 64)
            jac[to, 0:1024] = ref[0:64, :]
            jac[to, 1024:2048] = ref[64:128, :]
    for k in range(2):
        both[k * 256 : (k + 1) * 256, 0:1024] = sens[k][...]
        both[k * 256 : (k + 1) * 256, 1024:2048] = sens_got[k][...]
    value = lax.dot_general(
        jac[...], both[...], (((1,), (1,)), ((), ())), preferred_element_type=F32
    )
    for d in range(X):
        parts[source(d)] = value[:, d * 128 : (d + 1) * 128].astype(BF16)


def final_kernel(got, out):
    total = got[0].astype(F32)
    for k in range(1, X * L * Z):
        total += got[k].astype(F32)
    out[...] = total * (1.0 / math.sqrt(PARAMS))


def assemble_kernel(*refs):
    pieces, out, sems = refs[:X], refs[X], refs[X + 1]
    copies = []
    for d in range(X):
        at = lax.rem(lax.axis_index("x") + d, X)
        copies.append((pieces[d], out.at[:, pl.ds(pl.multiple_of(at * 1024, 1024), 1024)]))
    run_copies(copies, sems)


def ring(d):
    return [(x, (x + d) % X) for x in range(X)]


def over(value, axes):
    return lax.all_to_all(value, axes, split_axis=0, concat_axis=0, tiled=True)


def dma(n):
    return [pltpu.SemaphoreType.DMA((n,))]


def swap_rest(first, first_row, rows, behind):
    joined = call(
        functools.partial(join_kernel, first_row, rows),
        shape(X - 1, rows, 1024),
        first[1:],
        ANY,
        dma(X - 1),
        nbytes=2 * MIB,
        behind=behind,
    )
    return lax.ppermute(joined, "h", SWAP)


def body(jacobian, cov_rows, sens_carry):
    give = call(give_kernel, shape(64, 4096), (jacobian,), ANY, dma(2), nbytes=MIB)
    got = lax.ppermute(give, "c", SWAP)
    *packed, panel = call(
        pack_kernel,
        [shape(192, 1024)] * X + [shape(16, 16, 128)],
        (jacobian, got, cov_rows),
        ANY,
        dma(4 * X) + dma(16),
        nbytes=4 * MIB,
    )
    own_got = lax.ppermute(packed[0], "h", SWAP)
    first = [packed[0]] + [lax.ppermute(packed[d], "x", ring(d)) for d in range(1, X)]
    mine = over(panel, ("l", "z"))[0]
    panel = over(jnp.broadcast_to(mine, (32, 16, 128)), ("l", "z", "c"))
    panels = [panel] + [lax.ppermute(panel, "x", ring(d)) for d in range(1, X)]
    packed = call(
        carry_kernel, [shape(128, 1024)] * X, (sens_carry,), ANY, dma(X), nbytes=2 * MIB
    )
    carry = [packed[0]] + [lax.ppermute(packed[d], "x", ring(d)) for d in range(1, X)]
    cov_got = swap_rest(first, 128, 64, (own_got, panel))
    jac_got = swap_rest(first, 0, 128, (cov_got,))
    *sens, low, high = call(
        sens_kernel,
        [shape(128, 1024)] * X + [shape(256, 1024)] * 2,
        (*first, *carry, *panels, own_got, cov_got),
        VMEM,
        [pltpu.VMEM((512, 1024), BF16), pltpu.VMEM((512, WIDTH), BF16)],
        flops=2 * 512 * 512 * 1024,
        nbytes=2 * MIB,
        vmem=12,
    )
    sens_back = [sens[0]] + [lax.ppermute(sens[d], "x", ring(-d)) for d in range(1, X)]
    sens_got = [lax.ppermute(pair, "c", SWAP) for pair in (low, high)]
    parts = call(
        innov_kernel,
        shape(X, 512, 128),
        (own_got, jac_got, *first, low, high, *sens_got),
        VMEM,
        [pltpu.VMEM((512, 2048), BF16)] * 2,
        flops=2 * 512 * 512 * 2048,
        nbytes=2 * MIB,
        vmem=16,
        behind=sens_back[1:],
    )
    shared = over(parts.reshape(X * L * Z, 32, 128), ("x", "l", "z"))
    innovation = call(final_kernel, shape(32, 128, kind=F32), (shared,), VMEM, nbytes=2**19, vmem=4)
    sensitivity = call(
        assemble_kernel, shape(128, 4096), sens_back, ANY, dma(X), nbytes=2 * MIB
    )
    return (sensitivity, innovation.T)


def solution(mesh):
    fine = Mesh(mesh.devices.reshape(X, H, L, Z, C), AXES)
    spec = P(("x", "h"), ("l", "z", "c"))
    return jax.shard_map(
        body, mesh=fine, in_specs=(spec,) * 3, out_specs=(spec,) * 2, check_vma=False
    )
```

```python
import functools
import math

import jax
import jax.numpy as jnp
from jax import lax
from jax.experimental import pallas as pl
from jax.experimental.pallas import tpu as pltpu
from jax.sharding import Mesh, PartitionSpec as P

PARAMS = 131072
WIDTH = 512
X, H, L, Z, C = 4, 2, 2, 8, 2
AXES = ("x", "h", "l", "z", "c")
ANY = pl.BlockSpec(memory_space=pl.ANY)
VMEM = pl.BlockSpec(memory_space=pltpu.VMEM)
BF16, F32 = jnp.bfloat16, jnp.float32
SWAP = [(0, 1), (1, 0)]
MIB = 2**20


def source(d):
    return lax.rem(lax.axis_index("x") + X - d, X)


def call(kernel, outs, ins, spec, scratch=(), flops=0, nbytes=0, vmem=1, behind=()):
    return pl.pallas_call(
        kernel,
        out_shape=outs,
        in_specs=[spec] * len(ins) + [ANY] * len(behind),
        out_specs=jax.tree.map(lambda _: spec, outs),
        scratch_shapes=list(scratch),
        cost_estimate=pl.CostEstimate(flops=flops, bytes_accessed=nbytes, transcendentals=0),
        compiler_params=pltpu.CompilerParams(vmem_limit_bytes=vmem * MIB),
    )(*ins, *behind)


def shape(*dims, kind=BF16):
    return jax.ShapeDtypeStruct(dims, kind)


def run_copies(copies, sems):
    started = [pltpu.make_async_copy(a, b, sems.at[k]) for k, (a, b) in enumerate(copies)]
    for copy in started:
        copy.start()
    for copy in started:
        copy.wait()


def slab(half, core):
    return pl.ds(pl.multiple_of(half * 64 + core * 32, 32), 32)


def give_kernel(jac, give, panel, sems):
    other = 1 - lax.axis_index("c")
    copies = [(jac.at[slab(k, other), :], give.at[pl.ds(k * 32, 32), :]) for k in range(2)]
    for k in range(8):
        for n in range(4):
            copies.append((jac.at[pl.ds(k * 16, 16), pl.ds(n * 128, 128)], panel.at[k * 4 + n]))
    run_copies(copies, sems)


def part(d):
    at = lax.rem(lax.axis_index("x") + d, X)
    return pl.ds(pl.multiple_of(at * 1024, 1024), 1024)


def pack_kernel(jac, got, cov, carry, *refs):
    outs, sems = refs[:X], refs[X]
    core = lax.axis_index("c")
    copies = []
    for d in range(X):
        copies += [(jac.at[slab(n, core), part(d)], outs[d].at[pl.ds(n * 32, 32), :]) for n in range(2)]
        copies.append((got.at[:, part(d)], outs[d].at[pl.ds(64, 64), :]))
        copies.append((cov.at[:, part(d)], outs[d].at[pl.ds(128, 64), :]))
        copies.append((carry.at[:, part(d)], outs[d].at[pl.ds(192, 128), :]))
    run_copies(copies, sems)


def join_kernel(first_row, rows, *refs):
    pieces, out, sems = refs[: X - 1], refs[-2], refs[-1]
    run_copies(
        [(pieces[d].at[pl.ds(first_row, rows), :], out.at[d]) for d in range(X - 1)], sems
    )


def sens_kernel(*refs):
    first, panels, (own_got, cov_got) = refs[:4], refs[4:8], refs[8:10]
    outs, pairs, cov, panel = refs[10:14], refs[14:16], refs[16], refs[17]
    h = lax.axis_index("h")

    def rows(d, side):
        return pl.ds(pl.multiple_of((source(d) * H + side) * 64, 64), 64)

    for d in range(X):
        cov[rows(d, h), :] = first[d][128:192, :]
        cov[rows(d, 1 - h), :] = cov_got[d - 1] if d else own_got[128:192, :]
    for d in range(X):
        for k in range(8):
            for n in range(4):
                at = d * 128 + k * 16
                panel[at : at + 16, n * 128 : n * 128 + 128] = panels[d][k * 4 + n]
    for d in range(X):
        product = jnp.dot(
            panel[d * 128 : (d + 1) * 128, :], cov[...], preferred_element_type=F32
        )
        value = first[d][192:320, :].astype(F32) + product * (1.0 / math.sqrt(WIDTH))
        value = value.astype(BF16)
        outs[d][...] = value
        pairs[d // 2][d % 2 * 128 : d % 2 * 128 + 128, :] = value


def innov_kernel(own_got, jac_got, *refs):
    first, sens, sens_got = refs[:X], refs[X : X + 2], refs[X + 2 : X + 4]
    parts, jac, both = refs[-3:]
    h = lax.axis_index("h")
    for d in range(X):
        for side, ref in ((h, first[d]), (1 - h, jac_got.at[d - 1] if d else own_got)):
            to = pl.ds(pl.multiple_of((source(d) * H + side) * 64, 64), 64)
            jac[to, 0:1024] = ref[0:64, :]
            jac[to, 1024:2048] = ref[64:128, :]
    for k in range(2):
        both[k * 256 : (k + 1) * 256, 0:1024] = sens[k][...]
        both[k * 256 : (k + 1) * 256, 1024:2048] = sens_got[k][...]
    value = lax.dot_general(
        jac[...], both[...], (((1,), (1,)), ((), ())), preferred_element_type=F32
    )
    for d in range(X):
        parts[source(d)] = value[:, d * 128 : (d + 1) * 128].astype(BF16)


def final_kernel(got, out):
    total = got[0].astype(F32)
    for k in range(1, X * L * Z):
        total += got[k].astype(F32)
    out[...] = total * (1.0 / math.sqrt(PARAMS))


def assemble_kernel(*refs):
    pieces, out, sems = refs[:X], refs[X], refs[X + 1]
    copies = []
    for d in range(X):
        at = lax.rem(lax.axis_index("x") + d, X)
        copies.append((pieces[d], out.at[:, pl.ds(pl.multiple_of(at * 1024, 1024), 1024)]))
    run_copies(copies, sems)


def ring(d):
    return [(x, (x + d) % X) for x in range(X)]


def over(value, axes):
    return lax.all_to_all(value, axes, split_axis=0, concat_axis=0, tiled=True)


def dma(n):
    return [pltpu.SemaphoreType.DMA((n,))]


def swap_rest(first, first_row, rows, behind):
    joined = call(
        functools.partial(join_kernel, first_row, rows),
        shape(X - 1, rows, 1024),
        first[1:],
        ANY,
        dma(X - 1),
        nbytes=2 * MIB,
        behind=behind,
    )
    return lax.ppermute(joined, "h", SWAP)


def body(jacobian, cov_rows, sens_carry):
    give, panel = call(
        give_kernel,
        [shape(64, 4096), shape(32, 16, 128)],
        (jacobian,),
        ANY,
        dma(34),
        nbytes=MIB,
    )
    got = lax.ppermute(give, "c", SWAP)
    mine = over(panel, ("l", "z", "c"))[0]
    panel = over(jnp.broadcast_to(mine, (32, 16, 128)), ("l", "z", "c"))
    packed = call(
        pack_kernel,
        [shape(320, 1024)] * X,
        (jacobian, got, cov_rows, sens_carry),
        ANY,
        dma(5 * X),
        nbytes=5 * MIB,
    )
    own_got = lax.ppermute(packed[0][:192], "h", SWAP)
    first = [packed[0]] + [lax.ppermute(packed[d], "x", ring(d)) for d in range(1, X)]
    panels = [panel] + [lax.ppermute(panel, "x", ring(d)) for d in range(1, X)]
    cov_got = swap_rest(first, 128, 64, (own_got, panel))
    jac_got = swap_rest(first, 0, 128, (cov_got, *panels[1:]))
    *sens, low, high = call(
        sens_kernel,
        [shape(128, 1024)] * X + [shape(256, 1024)] * 2,
        (*first, *panels, own_got, cov_got),
        VMEM,
        [pltpu.VMEM((512, 1024), BF16), pltpu.VMEM((512, WIDTH), BF16)],
        flops=2 * 512 * 512 * 1024,
        nbytes=2 * MIB,
        vmem=12,
    )
    sens_back = [sens[0]] + [lax.ppermute(sens[d], "x", ring(-d)) for d in range(1, X)]
    sens_got = [lax.ppermute(pair, "c", SWAP) for pair in (low, high)]
    parts = call(
        innov_kernel,
        shape(X, 512, 128),
        (own_got, jac_got, *first, low, high, *sens_got),
        VMEM,
        [pltpu.VMEM((512, 2048), BF16)] * 2,
        flops=2 * 512 * 512 * 2048,
        nbytes=2 * MIB,
        vmem=16,
        behind=sens_back[1:],
    )
    shared = over(parts.reshape(X * L * Z, 32, 128), ("x", "l", "z"))
    innovation = call(final_kernel, shape(32, 128, kind=F32), (shared,), VMEM, nbytes=2**19, vmem=4)
    sensitivity = call(
        assemble_kernel, shape(128, 4096), sens_back, ANY, dma(X), nbytes=2 * MIB
    )
    return (sensitivity, innovation.T)


def solution(mesh):
    fine = Mesh(mesh.devices.reshape(X, H, L, Z, C), AXES)
    spec = P(("x", "h"), ("l", "z", "c"))
    return jax.shard_map(
        body, mesh=fine, in_specs=(spec,) * 3, out_specs=(spec,) * 2, check_vma=False
    )
```

```python
import functools
import math

import jax
import jax.numpy as jnp
from jax import lax
from jax.experimental import pallas as pl
from jax.experimental.pallas import tpu as pltpu
from jax.sharding import Mesh, PartitionSpec as P

PARAMS = 131072
WIDTH = 512
X, H, L, Z, C = 4, 2, 2, 8, 2
AXES = ("x", "h", "l", "z", "c")
ANY = pl.BlockSpec(memory_space=pl.ANY)
VMEM = pl.BlockSpec(memory_space=pltpu.VMEM)
BF16, F32 = jnp.bfloat16, jnp.float32
SWAP = [(0, 1), (1, 0)]
MIB = 2**20


def source(d):
    return lax.rem(lax.axis_index("x") + X - d, X)


def call(kernel, outs, ins, spec, scratch=(), flops=0, nbytes=0, vmem=1, behind=()):
    return pl.pallas_call(
        kernel,
        out_shape=outs,
        in_specs=[spec] * len(ins) + [ANY] * len(behind),
        out_specs=jax.tree.map(lambda _: spec, outs),
        scratch_shapes=list(scratch),
        cost_estimate=pl.CostEstimate(flops=flops, bytes_accessed=nbytes, transcendentals=0),
        compiler_params=pltpu.CompilerParams(vmem_limit_bytes=vmem * MIB),
    )(*ins, *behind)


def shape(*dims, kind=BF16):
    return jax.ShapeDtypeStruct(dims, kind)


def run_copies(copies, sems):
    started = [pltpu.make_async_copy(a, b, sems.at[k]) for k, (a, b) in enumerate(copies)]
    for copy in started:
        copy.start()
    for copy in started:
        copy.wait()


def slab(half, core):
    return pl.ds(pl.multiple_of(half * 64 + core * 32, 32), 32)


def give_kernel(jac, give, panel, sems):
    other = 1 - lax.axis_index("c")
    copies = [(jac.at[slab(k, other), :], give.at[pl.ds(k * 32, 32), :]) for k in range(2)]
    for k in range(8):
        for n in range(4):
            copies.append((jac.at[pl.ds(k * 16, 16), pl.ds(n * 128, 128)], panel.at[k * 4 + n]))
    run_copies(copies, sems)


def part(d):
    at = lax.rem(lax.axis_index("x") + d, X)
    return pl.ds(pl.multiple_of(at * 1024, 1024), 1024)


def pack_kernel(jac, got, cov, *refs):
    outs, sems = refs[:X], refs[X]
    core = lax.axis_index("c")
    copies = []
    for d in range(X):
        copies += [(jac.at[slab(n, core), part(d)], outs[d].at[pl.ds(n * 32, 32), :]) for n in range(2)]
        copies.append((got.at[:, part(d)], outs[d].at[pl.ds(64, 64), :]))
        copies.append((cov.at[:, part(d)], outs[d].at[pl.ds(128, 64), :]))
    run_copies(copies, sems)


def carry_kernel(carry, *refs):
    run_copies([(carry.at[:, part(d)], refs[d]) for d in range(X)], refs[X])


def join_kernel(first_row, rows, *refs):
    pieces, out, sems = refs[: X - 1], refs[-2], refs[-1]
    run_copies(
        [(pieces[d].at[pl.ds(first_row, rows), :], out.at[d]) for d in range(X - 1)], sems
    )


def sens_kernel(*refs):
    first, carry, panels, (own_got, cov_got) = refs[:4], refs[4:8], refs[8:12], refs[12:14]
    outs, pairs, cov, panel = refs[14:18], refs[18:20], refs[20], refs[21]
    h = lax.axis_index("h")

    def rows(d, side):
        return pl.ds(pl.multiple_of((source(d) * H + side) * 64, 64), 64)

    for d in range(X):
        cov[rows(d, h), :] = first[d][128:192, :]
        cov[rows(d, 1 - h), :] = cov_got[d - 1] if d else own_got[128:192, :]
    for d in range(X):
        for k in range(8):
            for n in range(4):
                at = d * 128 + k * 16
                panel[at : at + 16, n * 128 : n * 128 + 128] = panels[d][k * 4 + n]
    for d in range(X):
        product = jnp.dot(
            panel[d * 128 : (d + 1) * 128, :], cov[...], preferred_element_type=F32
        )
        value = carry[d][...].astype(F32) + product * (1.0 / math.sqrt(WIDTH))
        value = value.astype(BF16)
        outs[d][...] = value
        pairs[d // 2][d % 2 * 128 : d % 2 * 128 + 128, :] = value


def innov_kernel(own_got, jac_got, *refs):
    first, sens, sens_got = refs[:X], refs[X : X + 2], refs[X + 2 : X + 4]
    parts, jac, both = refs[-3:]
    h = lax.axis_index("h")
    for d in range(X):
        for side, ref in ((h, first[d]), (1 - h, jac_got.at[d - 1] if d else own_got)):
            to = pl.ds(pl.multiple_of((source(d) * H + side) * 64, 64), 64)
            jac[to, 0:1024] = ref[0:64, :]
            jac[to, 1024:2048] = ref[64:128, :]
    for k in range(2):
        both[k * 256 : (k + 1) * 256, 0:1024] = sens[k][...]
        both[k * 256 : (k + 1) * 256, 1024:2048] = sens_got[k][...]
    value = lax.dot_general(
        jac[...], both[...], (((1,), (1,)), ((), ())), preferred_element_type=F32
    )
    for d in range(X):
        parts[source(d)] = value[:, d * 128 : (d + 1) * 128].astype(BF16)


def final_kernel(got, out):
    total = got[0].astype(F32)
    for k in range(1, X * L * Z):
        total += got[k].astype(F32)
    out[...] = total * (1.0 / math.sqrt(PARAMS))


def assemble_kernel(*refs):
    pieces, out, sems = refs[:X], refs[X], refs[X + 1]
    copies = []
    for d in range(X):
        at = lax.rem(lax.axis_index("x") + d, X)
        copies.append((pieces[d], out.at[:, pl.ds(pl.multiple_of(at * 1024, 1024), 1024)]))
    run_copies(copies, sems)


def ring(d):
    return [(x, (x + d) % X) for x in range(X)]


def over(value, axes):
    return lax.all_to_all(value, axes, split_axis=0, concat_axis=0, tiled=True)


def dma(n):
    return [pltpu.SemaphoreType.DMA((n,))]


def join(first, first_row, rows, behind):
    return call(
        functools.partial(join_kernel, first_row, rows),
        shape(X - 1, rows, 1024),
        first[1:],
        ANY,
        dma(X - 1),
        nbytes=2 * MIB,
        behind=behind,
    )

def body(jacobian, cov_rows, sens_carry):
    give, panel = call(
        give_kernel,
        [shape(64, 4096), shape(32, 16, 128)],
        (jacobian,),
        ANY,
        dma(34),
        nbytes=MIB,
    )
    got = lax.ppermute(give, "c", SWAP)
    mine = over(panel, ("l", "z", "c"))[0]
    panel = over(jnp.broadcast_to(mine, (32, 16, 128)), ("l", "z", "c"))
    packed = call(
        pack_kernel,
        [shape(192, 1024)] * X,
        (jacobian, got, cov_rows),
        ANY,
        dma(4 * X),
        nbytes=4 * MIB,
    )
    own_got = lax.ppermute(packed[0], "h", SWAP)
    first = [packed[0]] + [lax.ppermute(packed[d], "x", ring(d)) for d in range(1, X)]
    panels = [panel] + [lax.ppermute(panel, "x", ring(d)) for d in range(1, X)]
    packed = call(
        carry_kernel, [shape(128, 1024)] * X, (sens_carry,), ANY, dma(X), nbytes=2 * MIB
    )
    carry = [packed[0]] + [lax.ppermute(packed[d], "x", ring(d)) for d in range(1, X)]
    cov_rest = join(first, 128, 64, (own_got, panel))
    jac_rest = join(first, 0, 128, (cov_rest,))
    cov_got = lax.ppermute(cov_rest, "h", SWAP)
    jac_got = lax.ppermute(jac_rest, "h", SWAP)
    *sens, low, high = call(
        sens_kernel,
        [shape(128, 1024)] * X + [shape(256, 1024)] * 2,
        (*first, *carry, *panels, own_got, cov_got),
        VMEM,
        [pltpu.VMEM((512, 1024), BF16), pltpu.VMEM((512, WIDTH), BF16)],
        flops=2 * 512 * 512 * 1024,
        nbytes=2 * MIB,
        vmem=12,
    )
    sens_back = [sens[0]] + [lax.ppermute(sens[d], "x", ring(-d)) for d in range(1, X)]
    sens_got = [lax.ppermute(pair, "c", SWAP) for pair in (low, high)]
    parts = call(
        innov_kernel,
        shape(X, 512, 128),
        (own_got, jac_got, *first, low, high, *sens_got),
        VMEM,
        [pltpu.VMEM((512, 2048), BF16)] * 2,
        flops=2 * 512 * 512 * 2048,
        nbytes=2 * MIB,
        vmem=16,
    )
    shared = over(parts.reshape(X * L * Z, 32, 128), ("x", "l", "z"))
    innovation = call(final_kernel, shape(32, 128, kind=F32), (shared,), VMEM, nbytes=2**19, vmem=4)
    sensitivity = call(
        assemble_kernel, shape(128, 4096), sens_back, ANY, dma(X), nbytes=2 * MIB
    )
    return (sensitivity, innovation.T)


def solution(mesh):
    fine = Mesh(mesh.devices.reshape(X, H, L, Z, C), AXES)
    spec = P(("x", "h"), ("l", "z", "c"))
    return jax.shard_map(
        body, mesh=fine, in_specs=(spec,) * 3, out_specs=(spec,) * 2, check_vma=False
    )
```

```python
import functools
import math

import jax
import jax.numpy as jnp
from jax import lax
from jax.experimental import pallas as pl
from jax.experimental.pallas import tpu as pltpu
from jax.sharding import Mesh, PartitionSpec as P

PARAMS = 131072
WIDTH = 512
X, H, L, Z, C = 4, 2, 2, 8, 2
AXES = ("x", "h", "l", "z", "c")
ANY = pl.BlockSpec(memory_space=pl.ANY)
VMEM = pl.BlockSpec(memory_space=pltpu.VMEM)
BF16, F32 = jnp.bfloat16, jnp.float32
SWAP = [(0, 1), (1, 0)]
MIB = 2**20


def source(d):
    return lax.rem(lax.axis_index("x") + X - d, X)


def call(kernel, outs, ins, spec, scratch=(), flops=0, nbytes=0, vmem=1, behind=()):
    return pl.pallas_call(
        kernel,
        out_shape=outs,
        in_specs=[spec] * len(ins) + [ANY] * len(behind),
        out_specs=jax.tree.map(lambda _: spec, outs),
        scratch_shapes=list(scratch),
        cost_estimate=pl.CostEstimate(flops=flops, bytes_accessed=nbytes, transcendentals=0),
        compiler_params=pltpu.CompilerParams(vmem_limit_bytes=vmem * MIB),
    )(*ins, *behind)


def shape(*dims, kind=BF16):
    return jax.ShapeDtypeStruct(dims, kind)


def run_copies(copies, sems):
    started = [pltpu.make_async_copy(a, b, sems.at[k]) for k, (a, b) in enumerate(copies)]
    for copy in started:
        copy.start()
    for copy in started:
        copy.wait()


def slab(half, core):
    return pl.ds(pl.multiple_of(half * 64 + core * 32, 32), 32)


def give_kernel(jac, give, panel, sems):
    other = 1 - lax.axis_index("c")
    copies = [(jac.at[slab(k, other), :], give.at[pl.ds(k * 32, 32), :]) for k in range(2)]
    for k in range(8):
        for n in range(4):
            copies.append((jac.at[pl.ds(k * 16, 16), pl.ds(n * 128, 128)], panel.at[k * 4 + n]))
    run_copies(copies, sems)


def part(d):
    at = lax.rem(lax.axis_index("x") + d, X)
    return pl.ds(pl.multiple_of(at * 1024, 1024), 1024)


def pack_kernel(jac, got, cov, *refs):
    outs, sems = refs[:X], refs[X]
    core = lax.axis_index("c")
    copies = []
    for d in range(X):
        copies += [(jac.at[slab(n, core), part(d)], outs[d].at[pl.ds(n * 32, 32), :]) for n in range(2)]
        copies.append((got.at[:, part(d)], outs[d].at[pl.ds(64, 64), :]))
        copies.append((cov.at[:, part(d)], outs[d].at[pl.ds(128, 64), :]))
    run_copies(copies, sems)


def carry_kernel(carry, *refs):
    run_copies([(carry.at[:, part(d)], refs[d]) for d in range(X)], refs[X])


def join_kernel(first_row, rows, *refs):
    pieces, out, sems = refs[: X - 1], refs[-2], refs[-1]
    run_copies(
        [(pieces[d].at[pl.ds(first_row, rows), :], out.at[d]) for d in range(X - 1)], sems
    )


def sens_kernel(*refs):
    first, carry, panels, (own_got, cov_got) = refs[:4], refs[4:8], refs[8:12], refs[12:14]
    outs, pairs, cov, panel = refs[14:18], refs[18:20], refs[20], refs[21]
    h = lax.axis_index("h")

    def rows(d, side):
        return pl.ds(pl.multiple_of((source(d) * H + side) * 64, 64), 64)

    for d in range(X):
        cov[rows(d, h), :] = first[d][128:192, :]
        cov[rows(d, 1 - h), :] = cov_got[d - 1] if d else own_got[128:192, :]
    for d in range(X):
        for k in range(8):
            for n in range(4):
                at = d * 128 + k * 16
                panel[at : at + 16, n * 128 : n * 128 + 128] = panels[d][k * 4 + n]
    for d in range(X):
        product = jnp.dot(
            panel[d * 128 : (d + 1) * 128, :], cov[...], preferred_element_type=F32
        )
        value = carry[d][...].astype(F32) + product * (1.0 / math.sqrt(WIDTH))
        value = value.astype(BF16)
        outs[d][...] = value
        pairs[d // 2][d % 2 * 128 : d % 2 * 128 + 128, :] = value


def innov_kernel(own_got, jac_got, *refs):
    first, sens, sens_got = refs[:X], refs[X : X + 2], refs[X + 2 : X + 4]
    parts, jac, both = refs[-3:]
    h = lax.axis_index("h")
    for d in range(X):
        for side, ref in ((h, first[d]), (1 - h, jac_got.at[d - 1] if d else own_got)):
            to = pl.ds(pl.multiple_of((source(d) * H + side) * 64, 64), 64)
            jac[to, 0:1024] = ref[0:64, :]
            jac[to, 1024:2048] = ref[64:128, :]
    for k in range(2):
        both[k * 256 : (k + 1) * 256, 0:1024] = sens[k][...]
        both[k * 256 : (k + 1) * 256, 1024:2048] = sens_got[k][...]
    value = lax.dot_general(
        jac[...], both[...], (((1,), (1,)), ((), ())), preferred_element_type=F32
    )
    for d in range(X):
        parts[source(d)] = value[:, d * 128 : (d + 1) * 128].astype(BF16)


def final_kernel(got, out):
    total = got[0].astype(F32)
    for k in range(1, X * L * Z):
        total += got[k].astype(F32)
    out[...] = total * (1.0 / math.sqrt(PARAMS))


def assemble_kernel(*refs):
    pieces, out, sems = refs[:X], refs[X], refs[X + 1]
    copies = []
    for d in range(X):
        at = lax.rem(lax.axis_index("x") + d, X)
        copies.append((pieces[d], out.at[:, pl.ds(pl.multiple_of(at * 1024, 1024), 1024)]))
    run_copies(copies, sems)


def ring(d):
    return [(x, (x + d) % X) for x in range(X)]


def over(value, axes):
    return lax.all_to_all(value, axes, split_axis=0, concat_axis=0, tiled=True)


def dma(n):
    return [pltpu.SemaphoreType.DMA((n,))]


def join(first, first_row, rows, behind):
    return call(
        functools.partial(join_kernel, first_row, rows),
        shape(X - 1, rows, 1024),
        first[1:],
        ANY,
        dma(X - 1),
        nbytes=2 * MIB,
        behind=behind,
    )

def body(jacobian, cov_rows, sens_carry):
    give, panel = call(
        give_kernel,
        [shape(64, 4096), shape(32, 16, 128)],
        (jacobian,),
        ANY,
        dma(34),
        nbytes=MIB,
        vmem=60,
    )
    got = lax.ppermute(give, "c", SWAP)
    mine = over(panel, ("l", "z", "c"))[0]
    panel = over(jnp.broadcast_to(mine, (32, 16, 128)), ("l", "z", "c"))
    packed = call(
        pack_kernel,
        [shape(192, 1024)] * X,
        (jacobian, got, cov_rows),
        ANY,
        dma(4 * X),
        nbytes=4 * MIB,
        vmem=60,
    )
    own_got = lax.ppermute(packed[0], "h", SWAP)
    first = [packed[0]] + [lax.ppermute(packed[d], "x", ring(d)) for d in range(1, X)]
    panels = [panel] + [lax.ppermute(panel, "x", ring(d)) for d in range(1, X)]
    packed = call(
        carry_kernel, [shape(128, 1024)] * X, (sens_carry,), ANY, dma(X), nbytes=2 * MIB
    )
    carry = [packed[0]] + [lax.ppermute(packed[d], "x", ring(d)) for d in range(1, X)]
    cov_rest = join(first, 128, 64, (own_got, panel))
    jac_rest = join(first, 0, 128, (cov_rest,))
    cov_got = lax.ppermute(cov_rest, "h", SWAP)
    jac_got = lax.ppermute(jac_rest, "h", SWAP)
    *sens, low, high = call(
        sens_kernel,
        [shape(128, 1024)] * X + [shape(256, 1024)] * 2,
        (*first, *carry, *panels, own_got, cov_got),
        VMEM,
        [pltpu.VMEM((512, 1024), BF16), pltpu.VMEM((512, WIDTH), BF16)],
        flops=2 * 512 * 512 * 1024,
        nbytes=2 * MIB,
        vmem=12,
    )
    sens_back = [sens[0]] + [lax.ppermute(sens[d], "x", ring(-d)) for d in range(1, X)]
    sens_got = [lax.ppermute(pair, "c", SWAP) for pair in (low, high)]
    parts = call(
        innov_kernel,
        shape(X, 512, 128),
        (own_got, jac_got, *first, low, high, *sens_got),
        VMEM,
        [pltpu.VMEM((512, 2048), BF16)] * 2,
        flops=2 * 512 * 512 * 2048,
        nbytes=2 * MIB,
        vmem=16,
        behind=(sens_back[1], sens_back[3]),
    )
    shared = over(parts.reshape(X * L * Z, 32, 128), ("x", "l", "z"))
    innovation = call(final_kernel, shape(32, 128, kind=F32), (shared,), VMEM, nbytes=2**19, vmem=4)
    sensitivity = call(
        assemble_kernel, shape(128, 4096), sens_back, ANY, dma(X), nbytes=2 * MIB
    )
    return (sensitivity, innovation.T)


def solution(mesh):
    fine = Mesh(mesh.devices.reshape(X, H, L, Z, C), AXES)
    spec = P(("x", "h"), ("l", "z", "c"))
    return jax.shard_map(
        body, mesh=fine, in_specs=(spec,) * 3, out_specs=(spec,) * 2, check_vma=False
    )
```

```python
import functools
import math

import jax
import jax.numpy as jnp
from jax import lax
from jax.experimental import pallas as pl
from jax.experimental.pallas import tpu as pltpu
from jax.sharding import Mesh, PartitionSpec as P

PARAMS = 131072
WIDTH = 512
X, H, L, Z, C = 4, 2, 2, 8, 2
AXES = ("x", "h", "l", "z", "c")
ANY = pl.BlockSpec(memory_space=pl.ANY)
VMEM = pl.BlockSpec(memory_space=pltpu.VMEM)
BF16, F32 = jnp.bfloat16, jnp.float32
SWAP = [(0, 1), (1, 0)]
MIB = 2**20


def source(d):
    return lax.rem(lax.axis_index("x") + X - d, X)


def call(kernel, outs, ins, spec, scratch=(), flops=0, nbytes=0, vmem=1, behind=(), outs_spec=None):
    return pl.pallas_call(
        kernel,
        out_shape=outs,
        in_specs=[spec] * len(ins) + [ANY] * len(behind),
        out_specs=jax.tree.map(lambda _: outs_spec or spec, outs),
        scratch_shapes=list(scratch),
        cost_estimate=pl.CostEstimate(flops=flops, bytes_accessed=nbytes, transcendentals=0),
        compiler_params=pltpu.CompilerParams(vmem_limit_bytes=vmem * MIB),
    )(*ins, *behind)


def shape(*dims, kind=BF16):
    return jax.ShapeDtypeStruct(dims, kind)


def run_copies(copies, sems):
    started = [pltpu.make_async_copy(a, b, sems.at[k]) for k, (a, b) in enumerate(copies)]
    for copy in started:
        copy.start()
    for copy in started:
        copy.wait()


def slab(half, core):
    return pl.ds(pl.multiple_of(half * 64 + core * 32, 32), 32)


def give_kernel(jac, give, panel, sems):
    other = 1 - lax.axis_index("c")
    copies = [(jac.at[slab(k, other), :], give.at[pl.ds(k * 32, 32), :]) for k in range(2)]
    for k in range(8):
        for n in range(4):
            copies.append((jac.at[pl.ds(k * 16, 16), pl.ds(n * 128, 128)], panel.at[k * 4 + n]))
    run_copies(copies, sems)


def part(d):
    at = lax.rem(lax.axis_index("x") + d, X)
    return pl.ds(pl.multiple_of(at * 1024, 1024), 1024)


def pack_kernel(jac, got, cov, *refs):
    outs, sems = refs[:X], refs[X]
    core = lax.axis_index("c")
    copies = []
    for d in range(X):
        copies += [(jac.at[slab(n, core), part(d)], outs[d].at[pl.ds(n * 32, 32), :]) for n in range(2)]
        copies.append((got.at[:, part(d)], outs[d].at[pl.ds(64, 64), :]))
        copies.append((cov.at[:, part(d)], outs[d].at[pl.ds(128, 64), :]))
    run_copies(copies, sems)


def carry_kernel(carry, *refs):
    run_copies([(carry.at[:, part(d)], refs[d]) for d in range(X)], refs[X])


def join_kernel(first_row, rows, *refs):
    pieces, out, sems = refs[: X - 1], refs[-2], refs[-1]
    run_copies(
        [(pieces[d].at[pl.ds(first_row, rows), :], out.at[d]) for d in range(X - 1)], sems
    )


def sens_kernel(*refs):
    first, carry, panels, (own_got, cov_got) = refs[:4], refs[4:8], refs[8:12], refs[12:14]
    outs, pairs, cov, panel = refs[14:18], refs[18:20], refs[20], refs[21]
    h = lax.axis_index("h")

    def rows(d, side):
        return pl.ds(pl.multiple_of((source(d) * H + side) * 64, 64), 64)

    for d in range(X):
        cov[rows(d, h), :] = first[d][128:192, :]
        cov[rows(d, 1 - h), :] = cov_got[d - 1] if d else own_got[128:192, :]
    for d in range(X):
        for k in range(8):
            for n in range(4):
                at = d * 128 + k * 16
                panel[at : at + 16, n * 128 : n * 128 + 128] = panels[d][k * 4 + n]
    for d in range(X):
        product = jnp.dot(
            panel[d * 128 : (d + 1) * 128, :], cov[...], preferred_element_type=F32
        )
        value = carry[d][...].astype(F32) + product * (1.0 / math.sqrt(WIDTH))
        value = value.astype(BF16)
        outs[d][...] = value
        pairs[d // 2][d % 2 * 128 : d % 2 * 128 + 128, :] = value


def innov_kernel(own_got, jac_got, *refs):
    first, sens, sens_got = refs[:X], refs[X : X + 2], refs[X + 2 : X + 4]
    parts, jac, both = refs[-3:]
    h = lax.axis_index("h")
    for d in range(X):
        for side, ref in ((h, first[d]), (1 - h, jac_got.at[d - 1] if d else own_got)):
            to = pl.ds(pl.multiple_of((source(d) * H + side) * 64, 64), 64)
            jac[to, 0:1024] = ref[0:64, :]
            jac[to, 1024:2048] = ref[64:128, :]
    for k in range(2):
        both[k * 256 : (k + 1) * 256, 0:1024] = sens[k][...]
        both[k * 256 : (k + 1) * 256, 1024:2048] = sens_got[k][...]
    value = lax.dot_general(
        jac[...], both[...], (((1,), (1,)), ((), ())), preferred_element_type=F32
    )
    for d in range(X):
        parts[source(d)] = value[:, d * 128 : (d + 1) * 128].astype(BF16)


def final_kernel(got, out):
    total = got[0].astype(F32)
    for k in range(1, X * L * Z):
        total += got[k].astype(F32)
    out[...] = total * (1.0 / math.sqrt(PARAMS))


def assemble_kernel(*refs):
    pieces, out, sems = refs[:X], refs[X], refs[X + 1]
    copies = []
    for d in range(X):
        at = lax.rem(lax.axis_index("x") + d, X)
        copies.append((pieces[d], out.at[:, pl.ds(pl.multiple_of(at * 1024, 1024), 1024)]))
    run_copies(copies, sems)


def ring(d):
    return [(x, (x + d) % X) for x in range(X)]


def over(value, axes):
    return lax.all_to_all(value, axes, split_axis=0, concat_axis=0, tiled=True)


def dma(n):
    return [pltpu.SemaphoreType.DMA((n,))]


def join(first, first_row, rows, behind):
    return call(
        functools.partial(join_kernel, first_row, rows),
        shape(X - 1, rows, 1024),
        first[1:],
        ANY,
        dma(X - 1),
        nbytes=2 * MIB,
        behind=behind,
    )

def body(jacobian, cov_rows, sens_carry):
    give, panel = call(
        give_kernel,
        [shape(64, 4096), shape(32, 16, 128)],
        (jacobian,),
        VMEM,
        dma(34),
        outs_spec=ANY,
        nbytes=MIB,
        vmem=60,
    )
    got = lax.ppermute(give, "c", SWAP)
    mine = over(panel, ("l", "z", "c"))[0]
    panel = over(jnp.broadcast_to(mine, (32, 16, 128)), ("l", "z", "c"))
    packed = call(
        pack_kernel,
        [shape(192, 1024)] * X,
        (jacobian, got, cov_rows),
        VMEM,
        dma(4 * X),
        outs_spec=ANY,
        nbytes=4 * MIB,
        vmem=60,
    )
    own_got = lax.ppermute(packed[0], "h", SWAP)
    first = [packed[0]] + [lax.ppermute(packed[d], "x", ring(d)) for d in range(1, X)]
    panels = [panel] + [lax.ppermute(panel, "x", ring(d)) for d in range(1, X)]
    packed = call(
        carry_kernel, [shape(128, 1024)] * X, (sens_carry,), ANY, dma(X), nbytes=2 * MIB
    )
    carry = [packed[0]] + [lax.ppermute(packed[d], "x", ring(d)) for d in range(1, X)]
    cov_rest = join(first, 128, 64, (own_got, panel))
    jac_rest = join(first, 0, 128, (cov_rest,))
    cov_got = lax.ppermute(cov_rest, "h", SWAP)
    jac_got = lax.ppermute(jac_rest, "h", SWAP)
    *sens, low, high = call(
        sens_kernel,
        [shape(128, 1024)] * X + [shape(256, 1024)] * 2,
        (*first, *carry, *panels, own_got, cov_got),
        VMEM,
        [pltpu.VMEM((512, 1024), BF16), pltpu.VMEM((512, WIDTH), BF16)],
        flops=2 * 512 * 512 * 1024,
        nbytes=2 * MIB,
        vmem=12,
    )
    sens_back = [sens[0]] + [lax.ppermute(sens[d], "x", ring(-d)) for d in range(1, X)]
    sens_got = [lax.ppermute(pair, "c", SWAP) for pair in (low, high)]
    parts = call(
        innov_kernel,
        shape(X, 512, 128),
        (own_got, jac_got, *first, low, high, *sens_got),
        VMEM,
        [pltpu.VMEM((512, 2048), BF16)] * 2,
        flops=2 * 512 * 512 * 2048,
        nbytes=2 * MIB,
        vmem=16,
        behind=(sens_back[1], sens_back[2]),
    )
    shared = over(parts.reshape(X * L * Z, 32, 128), ("x", "l", "z"))
    innovation = call(final_kernel, shape(32, 128, kind=F32), (shared,), VMEM, nbytes=2**19, vmem=4)
    sensitivity = call(
        assemble_kernel, shape(128, 4096), sens_back, ANY, dma(X), nbytes=2 * MIB
    )
    return (sensitivity, innovation.T)


def solution(mesh):
    fine = Mesh(mesh.devices.reshape(X, H, L, Z, C), AXES)
    spec = P(("x", "h"), ("l", "z", "c"))
    return jax.shard_map(
        body, mesh=fine, in_specs=(spec,) * 3, out_specs=(spec,) * 2, check_vma=False
    )
```

```python
import functools
import math

import jax
import jax.numpy as jnp
from jax import lax
from jax.experimental import pallas as pl
from jax.experimental.pallas import tpu as pltpu
from jax.sharding import Mesh, PartitionSpec as P

PARAMS = 131072
WIDTH = 512
X, H, L, Z, C = 4, 2, 2, 8, 2
AXES = ("x", "h", "l", "z", "c")
ANY = pl.BlockSpec(memory_space=pl.ANY)
VMEM = pl.BlockSpec(memory_space=pltpu.VMEM)
BF16, F32 = jnp.bfloat16, jnp.float32
SWAP = [(0, 1), (1, 0)]
MIB = 2**20


def source(d):
    return lax.rem(lax.axis_index("x") + X - d, X)


def call(kernel, outs, ins, spec, scratch=(), flops=0, nbytes=0, vmem=1, behind=(), outs_spec=None):
    return pl.pallas_call(
        kernel,
        out_shape=outs,
        in_specs=[spec] * len(ins) + [ANY] * len(behind),
        out_specs=jax.tree.map(lambda _: outs_spec or spec, outs),
        scratch_shapes=list(scratch),
        cost_estimate=pl.CostEstimate(flops=flops, bytes_accessed=nbytes, transcendentals=0),
        compiler_params=pltpu.CompilerParams(vmem_limit_bytes=vmem * MIB),
    )(*ins, *behind)


def shape(*dims, kind=BF16):
    return jax.ShapeDtypeStruct(dims, kind)


def run_copies(copies, sems):
    started = [pltpu.make_async_copy(a, b, sems.at[k]) for k, (a, b) in enumerate(copies)]
    for copy in started:
        copy.start()
    for copy in started:
        copy.wait()


def slab(half, core):
    return pl.ds(pl.multiple_of(half * 64 + core * 32, 32), 32)


def give_kernel(jac, give, panel, sems):
    other = 1 - lax.axis_index("c")
    copies = [(jac.at[slab(k, other), :], give.at[pl.ds(k * 32, 32), :]) for k in range(2)]
    for k in range(8):
        for n in range(4):
            copies.append((jac.at[pl.ds(k * 16, 16), pl.ds(n * 128, 128)], panel.at[k * 4 + n]))
    run_copies(copies, sems)


def part(d):
    at = lax.rem(lax.axis_index("x") + d, X)
    return pl.ds(pl.multiple_of(at * 1024, 1024), 1024)


def pack_kernel(jac, got, cov, *refs):
    outs, sems = refs[:X], refs[X]
    core = lax.axis_index("c")
    copies = []
    for d in range(X):
        copies += [(jac.at[slab(n, core), part(d)], outs[d].at[pl.ds(n * 32, 32), :]) for n in range(2)]
        copies.append((got.at[:, part(d)], outs[d].at[pl.ds(64, 64), :]))
        copies.append((cov.at[:, part(d)], outs[d].at[pl.ds(128, 64), :]))
    run_copies(copies, sems)


def carry_kernel(carry, *refs):
    run_copies([(carry.at[:, part(d)], refs[d]) for d in range(X)], refs[X])


def join_kernel(first_row, rows, *refs):
    pieces, out, sems = refs[: X - 1], refs[-2], refs[-1]
    run_copies(
        [(pieces[d].at[pl.ds(first_row, rows), :], out.at[d]) for d in range(X - 1)], sems
    )


def sens_kernel(*refs):
    first, carry, panels, (own_got, cov_got) = refs[:4], refs[4:8], refs[8:12], refs[12:14]
    outs, pairs, cov, panel = refs[14:18], refs[18:20], refs[20], refs[21]
    h = lax.axis_index("h")

    def rows(d, side):
        return pl.ds(pl.multiple_of((source(d) * H + side) * 64, 64), 64)

    for d in range(X):
        cov[rows(d, h), :] = first[d][128:192, :]
        cov[rows(d, 1 - h), :] = cov_got[d - 1] if d else own_got[128:192, :]
    for d in range(X):
        for k in range(8):
            for n in range(4):
                at = d * 128 + k * 16
                panel[at : at + 16, n * 128 : n * 128 + 128] = panels[d][k * 4 + n]
    for d in range(X):
        product = jnp.dot(
            panel[d * 128 : (d + 1) * 128, :], cov[...], preferred_element_type=F32
        )
        value = carry[d][...].astype(F32) + product * (1.0 / math.sqrt(WIDTH))
        value = value.astype(BF16)
        outs[d][...] = value
        pairs[d // 2][d % 2 * 128 : d % 2 * 128 + 128, :] = value


def innov_kernel(own_got, jac_got, *refs):
    first, sens, sens_got = refs[:X], refs[X : X + 2], refs[X + 2 : X + 4]
    own, parts, jac, both = refs[-X - 2], refs[-X - 1 : -2], refs[-2], refs[-1]
    h = lax.axis_index("h")
    for d in range(X):
        for side, ref in ((h, first[d]), (1 - h, jac_got.at[d - 1] if d else own_got)):
            to = pl.ds(pl.multiple_of((source(d) * H + side) * 64, 64), 64)
            jac[to, 0:1024] = ref[0:64, :]
            jac[to, 1024:2048] = ref[64:128, :]
    for k in range(2):
        both[k * 256 : (k + 1) * 256, 0:1024] = sens[k][...]
        both[k * 256 : (k + 1) * 256, 1024:2048] = sens_got[k][...]
    value = lax.dot_general(
        jac[...], both[...], (((1,), (1,)), ((), ())), preferred_element_type=F32
    )
    own[...] = value[:, 0:128]
    for d in range(1, X):
        parts[d - 1][...] = value[:, d * 128 : (d + 1) * 128].astype(BF16)


def sum_kernel(own, *refs):
    total = own[...]
    for ref in refs[:-1]:
        total += ref[...].astype(F32)
    refs[-1][...] = total.astype(BF16)


def final_kernel(got, out):
    total = got[0].astype(F32)
    for k in range(1, L * Z):
        total += got[k].astype(F32)
    out[...] = total * (1.0 / math.sqrt(PARAMS))


def assemble_kernel(*refs):
    pieces, out, sems = refs[:X], refs[X], refs[X + 1]
    copies = []
    for d in range(X):
        at = lax.rem(lax.axis_index("x") + d, X)
        copies.append((pieces[d], out.at[:, pl.ds(pl.multiple_of(at * 1024, 1024), 1024)]))
    run_copies(copies, sems)


def ring(d):
    return [(x, (x + d) % X) for x in range(X)]


def over(value, axes):
    return lax.all_to_all(value, axes, split_axis=0, concat_axis=0, tiled=True)


def dma(n):
    return [pltpu.SemaphoreType.DMA((n,))]


def join(first, first_row, rows, behind):
    return call(
        functools.partial(join_kernel, first_row, rows),
        shape(X - 1, rows, 1024),
        first[1:],
        ANY,
        dma(X - 1),
        nbytes=2 * MIB,
        behind=behind,
    )

def body(jacobian, cov_rows, sens_carry):
    give, panel = call(
        give_kernel,
        [shape(64, 4096), shape(32, 16, 128)],
        (jacobian,),
        VMEM,
        dma(34),
        outs_spec=ANY,
        nbytes=MIB,
        vmem=60,
    )
    got = lax.ppermute(give, "c", SWAP)
    mine = over(panel, ("l", "z", "c"))[0]
    panel = over(jnp.broadcast_to(mine, (32, 16, 128)), ("l", "z", "c"))
    packed = call(
        pack_kernel,
        [shape(192, 1024)] * X,
        (jacobian, got, cov_rows),
        VMEM,
        dma(4 * X),
        outs_spec=ANY,
        nbytes=4 * MIB,
        vmem=60,
    )
    own_got = lax.ppermute(packed[0], "h", SWAP)
    first = [packed[0]] + [lax.ppermute(packed[d], "x", ring(d)) for d in range(1, X)]
    panels = [panel] + [lax.ppermute(panel, "x", ring(d)) for d in range(1, X)]
    packed = call(
        carry_kernel, [shape(128, 1024)] * X, (sens_carry,), ANY, dma(X), nbytes=2 * MIB
    )
    carry = [packed[0]] + [lax.ppermute(packed[d], "x", ring(d)) for d in range(1, X)]
    cov_rest = join(first, 128, 64, (own_got, panel))
    jac_rest = join(first, 0, 128, (cov_rest,))
    cov_got = lax.ppermute(cov_rest, "h", SWAP)
    jac_got = lax.ppermute(jac_rest, "h", SWAP)
    *sens, low, high = call(
        sens_kernel,
        [shape(128, 1024)] * X + [shape(256, 1024)] * 2,
        (*first, *carry, *panels, own_got, cov_got),
        VMEM,
        [pltpu.VMEM((512, 1024), BF16), pltpu.VMEM((512, WIDTH), BF16)],
        flops=2 * 512 * 512 * 1024,
        nbytes=2 * MIB,
        vmem=12,
    )
    sens_back = [sens[0]] + [lax.ppermute(sens[d], "x", ring(-d)) for d in range(1, X)]
    sens_got = [lax.ppermute(pair, "c", SWAP) for pair in (low, high)]
    own, *parts = call(
        innov_kernel,
        [shape(512, 128, kind=F32)] + [shape(512, 128)] * (X - 1),
        (own_got, jac_got, *first, low, high, *sens_got),
        VMEM,
        [pltpu.VMEM((512, 2048), BF16)] * 2,
        flops=2 * 512 * 512 * 2048,
        nbytes=2 * MIB,
        vmem=16,
        behind=(sens_back[1], sens_back[2]),
    )
    parts = [lax.ppermute(parts[d - 1], "x", ring(-d)) for d in range(1, X)]
    summed = call(sum_kernel, shape(512, 128), (own, *parts), VMEM, nbytes=MIB, vmem=4)
    shared = over(summed.reshape(L * Z, 32, 128), ("l", "z"))
    innovation = call(final_kernel, shape(32, 128, kind=F32), (shared,), VMEM, nbytes=2**19, vmem=4)
    sensitivity = call(
        assemble_kernel, shape(128, 4096), sens_back, ANY, dma(X), nbytes=2 * MIB
    )
    return (sensitivity, innovation.T)


def solution(mesh):
    fine = Mesh(mesh.devices.reshape(X, H, L, Z, C), AXES)
    spec = P(("x", "h"), ("l", "z", "c"))
    return jax.shard_map(
        body, mesh=fine, in_specs=(spec,) * 3, out_specs=(spec,) * 2, check_vma=False
    )
```

```python
import functools
import math

import jax
import jax.numpy as jnp
from jax import lax
from jax.experimental import pallas as pl
from jax.experimental.pallas import tpu as pltpu
from jax.sharding import Mesh, PartitionSpec as P

PARAMS = 131072
WIDTH = 512
X, H, L, Z, C = 4, 2, 2, 8, 2
AXES = ("x", "h", "l", "z", "c")
ANY = pl.BlockSpec(memory_space=pl.ANY)
VMEM = pl.BlockSpec(memory_space=pltpu.VMEM)
BF16, F32 = jnp.bfloat16, jnp.float32
SWAP = [(0, 1), (1, 0)]
MIB = 2**20


def source(d):
    return lax.rem(lax.axis_index("x") + X - d, X)


def call(kernel, outs, ins, spec, scratch=(), flops=0, nbytes=0, vmem=1, behind=(), aliases=None):
    return pl.pallas_call(
        kernel,
        out_shape=outs,
        in_specs=[spec] * len(ins) + [ANY] * len(behind),
        out_specs=jax.tree.map(lambda _: spec, outs),
        scratch_shapes=list(scratch),
        input_output_aliases=aliases or {},
        cost_estimate=pl.CostEstimate(flops=flops, bytes_accessed=nbytes, transcendentals=0),
        compiler_params=pltpu.CompilerParams(vmem_limit_bytes=vmem * MIB),
    )(*ins, *behind)


def shape(*dims, kind=BF16):
    return jax.ShapeDtypeStruct(dims, kind)


def run_copies(copies, sems):
    started = [pltpu.make_async_copy(a, b, sems.at[k]) for k, (a, b) in enumerate(copies)]
    for copy in started:
        copy.start()
    for copy in started:
        copy.wait()


def slab(half, core):
    return pl.ds(pl.multiple_of(half * 64 + core * 32, 32), 32)


def part(d):
    at = lax.rem(lax.axis_index("x") + d, X)
    return pl.ds(pl.multiple_of(at * 1024, 1024), 1024)


def give_kernel(jac, cov, give, panel, *refs):
    outs, sems = refs[:X], refs[X]
    core = lax.axis_index("c")
    copies = [(jac.at[slab(k, 1 - core), :], give.at[pl.ds(k * 32, 32), :]) for k in range(2)]
    for k in range(8):
        for n in range(4):
            copies.append((jac.at[pl.ds(k * 16, 16), pl.ds(n * 128, 128)], panel.at[k * 4 + n]))
    for d in range(X):
        copies += [(jac.at[slab(n, core), part(d)], outs[d].at[pl.ds(n * 32, 32), :]) for n in range(2)]
        copies.append((cov.at[:, part(d)], outs[d].at[pl.ds(128, 64), :]))
    run_copies(copies, sems)


def fill_kernel(got, *refs):
    outs, sems = refs[X : 2 * X], refs[2 * X]
    run_copies([(got.at[:, part(d)], outs[d].at[pl.ds(64, 64), :]) for d in range(X)], sems)


def carry_kernel(carry, *refs):
    run_copies([(carry.at[:, part(d)], refs[d]) for d in range(X)], refs[X])


def join_kernel(first_row, rows, *refs):
    pieces, out, sems = refs[: X - 1], refs[-2], refs[-1]
    run_copies(
        [(pieces[d].at[pl.ds(first_row, rows), :], out.at[d]) for d in range(X - 1)], sems
    )


def sens_kernel(*refs):
    first, carry, panels, (own_got, cov_got) = refs[:4], refs[4:8], refs[8:12], refs[12:14]
    outs, pairs, cov, panel = refs[14:18], refs[18:20], refs[20], refs[21]
    h = lax.axis_index("h")

    def rows(d, side):
        return pl.ds(pl.multiple_of((source(d) * H + side) * 64, 64), 64)

    for d in range(X):
        cov[rows(d, h), :] = first[d][128:192, :]
        cov[rows(d, 1 - h), :] = cov_got[d - 1] if d else own_got[128:192, :]
    for d in range(X):
        for k in range(8):
            for n in range(4):
                at = d * 128 + k * 16
                panel[at : at + 16, n * 128 : n * 128 + 128] = panels[d][k * 4 + n]
    for d in range(X):
        product = jnp.dot(
            panel[d * 128 : (d + 1) * 128, :], cov[...], preferred_element_type=F32
        )
        value = carry[d][...].astype(F32) + product * (1.0 / math.sqrt(WIDTH))
        value = value.astype(BF16)
        outs[d][...] = value
        pairs[d // 2][d % 2 * 128 : d % 2 * 128 + 128, :] = value


def innov_kernel(own_got, jac_got, *refs):
    first, sens, sens_got = refs[:X], refs[X : X + 2], refs[X + 2 : X + 4]
    parts, jac, both = refs[-3:]
    h = lax.axis_index("h")
    for d in range(X):
        for side, ref in ((h, first[d]), (1 - h, jac_got.at[d - 1] if d else own_got)):
            to = pl.ds(pl.multiple_of((source(d) * H + side) * 64, 64), 64)
            jac[to, 0:1024] = ref[0:64, :]
            jac[to, 1024:2048] = ref[64:128, :]
    for k in range(2):
        both[k * 256 : (k + 1) * 256, 0:1024] = sens[k][...]
        both[k * 256 : (k + 1) * 256, 1024:2048] = sens_got[k][...]
    value = lax.dot_general(
        jac[...], both[...], (((1,), (1,)), ((), ())), preferred_element_type=F32
    )
    for d in range(X):
        parts[source(d)] = value[:, d * 128 : (d + 1) * 128].astype(BF16)


def final_kernel(got, out):
    total = got[0].astype(F32)
    for k in range(1, X * L * Z):
        total += got[k].astype(F32)
    out[...] = total * (1.0 / math.sqrt(PARAMS))


def assemble_kernel(*refs):
    pieces, out, sems = refs[:X], refs[X], refs[X + 1]
    copies = []
    for d in range(X):
        at = lax.rem(lax.axis_index("x") + d, X)
        copies.append((pieces[d], out.at[:, pl.ds(pl.multiple_of(at * 1024, 1024), 1024)]))
    run_copies(copies, sems)


def ring(d):
    return [(x, (x + d) % X) for x in range(X)]


def over(value, axes):
    return lax.all_to_all(value, axes, split_axis=0, concat_axis=0, tiled=True)


def dma(n):
    return [pltpu.SemaphoreType.DMA((n,))]


def join(first, first_row, rows, behind):
    return call(
        functools.partial(join_kernel, first_row, rows),
        shape(X - 1, rows, 1024),
        first[1:],
        ANY,
        dma(X - 1),
        nbytes=2 * MIB,
        behind=behind,
    )

def body(jacobian, cov_rows, sens_carry):
    give, panel, *packed = call(
        give_kernel,
        [shape(64, 4096), shape(32, 16, 128)] + [shape(192, 1024)] * X,
        (jacobian, cov_rows),
        ANY,
        dma(34 + 3 * X),
        nbytes=4 * MIB,
    )
    got = lax.ppermute(give, "c", SWAP)
    mine = over(panel, ("l", "z", "c"))[0]
    panel = over(jnp.broadcast_to(mine, (32, 16, 128)), ("l", "z", "c"))
    packed = call(
        fill_kernel,
        [shape(192, 1024)] * X,
        (got, *packed),
        ANY,
        dma(X),
        nbytes=MIB,
        aliases={1 + d: d for d in range(X)},
    )
    own_got = lax.ppermute(packed[0], "h", SWAP)
    first = [packed[0]] + [lax.ppermute(packed[d], "x", ring(d)) for d in range(1, X)]
    panels = [panel] + [lax.ppermute(panel, "x", ring(d)) for d in range(1, X)]
    packed = call(
        carry_kernel, [shape(128, 1024)] * X, (sens_carry,), ANY, dma(X), nbytes=2 * MIB
    )
    carry = [packed[0]] + [lax.ppermute(packed[d], "x", ring(d)) for d in range(1, X)]
    cov_rest = join(first, 128, 64, (panel,))
    jac_rest = join(first, 0, 128, (cov_rest, own_got))
    cov_got = lax.ppermute(cov_rest, "h", SWAP)
    jac_got = lax.ppermute(jac_rest, "h", SWAP)
    *sens, low, high = call(
        sens_kernel,
        [shape(128, 1024)] * X + [shape(256, 1024)] * 2,
        (*first, *carry, *panels, own_got, cov_got),
        VMEM,
        [pltpu.VMEM((512, 1024), BF16), pltpu.VMEM((512, WIDTH), BF16)],
        flops=2 * 512 * 512 * 1024,
        nbytes=2 * MIB,
        vmem=12,
    )
    sens_back = [sens[0]] + [lax.ppermute(sens[d], "x", ring(-d)) for d in range(1, X)]
    sens_got = [lax.ppermute(pair, "c", SWAP) for pair in (low, high)]
    parts = call(
        innov_kernel,
        shape(X, 512, 128),
        (own_got, jac_got, *first, low, high, *sens_got),
        VMEM,
        [pltpu.VMEM((512, 2048), BF16)] * 2,
        flops=2 * 512 * 512 * 2048,
        nbytes=2 * MIB,
        vmem=16,
    )
    shared = over(parts.reshape(X * L * Z, 32, 128), ("x", "l", "z"))
    innovation = call(final_kernel, shape(32, 128, kind=F32), (shared,), VMEM, nbytes=2**19, vmem=4)
    sensitivity = call(
        assemble_kernel, shape(128, 4096), sens_back, ANY, dma(X), nbytes=2 * MIB
    )
    return (sensitivity, innovation.T)


def solution(mesh):
    fine = Mesh(mesh.devices.reshape(X, H, L, Z, C), AXES)
    spec = P(("x", "h"), ("l", "z", "c"))
    return jax.shard_map(
        body, mesh=fine, in_specs=(spec,) * 3, out_specs=(spec,) * 2, check_vma=False
    )
```

```python
import functools
import math

import jax
import jax.numpy as jnp
from jax import lax
from jax.experimental import pallas as pl
from jax.experimental.pallas import tpu as pltpu
from jax.sharding import Mesh, PartitionSpec as P

PARAMS = 131072
WIDTH = 512
X, H, L, Z, C = 4, 2, 2, 8, 2
AXES = ("x", "h", "l", "z", "c")
ANY = pl.BlockSpec(memory_space=pl.ANY)
VMEM = pl.BlockSpec(memory_space=pltpu.VMEM)
BF16, F32 = jnp.bfloat16, jnp.float32
SWAP = [(0, 1), (1, 0)]
MIB = 2**20


def source(d):
    return lax.rem(lax.axis_index("x") + X - d, X)


def call(kernel, outs, ins, spec, scratch=(), flops=0, nbytes=0, vmem=1, behind=(), aliases=None):
    return pl.pallas_call(
        kernel,
        out_shape=outs,
        in_specs=[spec] * len(ins) + [ANY] * len(behind),
        out_specs=jax.tree.map(lambda _: spec, outs),
        scratch_shapes=list(scratch),
        input_output_aliases=aliases or {},
        cost_estimate=pl.CostEstimate(flops=flops, bytes_accessed=nbytes, transcendentals=0),
        compiler_params=pltpu.CompilerParams(vmem_limit_bytes=vmem * MIB),
    )(*ins, *behind)


def shape(*dims, kind=BF16):
    return jax.ShapeDtypeStruct(dims, kind)


def run_copies(copies, sems):
    started = [pltpu.make_async_copy(a, b, sems.at[k]) for k, (a, b) in enumerate(copies)]
    for copy in started:
        copy.start()
    for copy in started:
        copy.wait()


def slab(half, core):
    return pl.ds(pl.multiple_of(half * 64 + core * 32, 32), 32)


def part(d):
    at = lax.rem(lax.axis_index("x") + d, X)
    return pl.ds(pl.multiple_of(at * 1024, 1024), 1024)


def give_kernel(jac, cov, give, panel, *refs):
    outs, sems = refs[:X], refs[X]
    core = lax.axis_index("c")
    copies = [(jac.at[slab(k, 1 - core), :], give.at[pl.ds(k * 32, 32), :]) for k in range(2)]
    for k in range(8):
        for n in range(4):
            copies.append((jac.at[pl.ds(k * 16, 16), pl.ds(n * 128, 128)], panel.at[k * 4 + n]))
    for d in range(X):
        copies += [(jac.at[slab(n, core), part(d)], outs[d].at[pl.ds(n * 32, 32), :]) for n in range(2)]
        copies.append((cov.at[:, part(d)], outs[d].at[pl.ds(128, 64), :]))
    run_copies(copies, sems)


def fill_kernel(got, *refs):
    outs, sems = refs[X : 2 * X], refs[2 * X]
    run_copies([(got.at[:, part(d)], outs[d].at[pl.ds(64, 64), :]) for d in range(X)], sems)


def carry_kernel(carry, *refs):
    run_copies([(carry.at[:, part(d)], refs[d]) for d in range(X)], refs[X])


def join_kernel(first_row, rows, *refs):
    pieces, out, sems = refs[: X - 1], refs[-2], refs[-1]
    run_copies(
        [(pieces[d].at[pl.ds(first_row, rows), :], out.at[d]) for d in range(X - 1)], sems
    )


def sens_kernel(*refs):
    first, carry, panels, (own_got, cov_got) = refs[:4], refs[4:8], refs[8:12], refs[12:14]
    outs, pairs, cov, panel = refs[14:18], refs[18:20], refs[20], refs[21]
    h = lax.axis_index("h")

    def rows(d, side):
        return pl.ds(pl.multiple_of((source(d) * H + side) * 64, 64), 64)

    for d in range(X):
        cov[rows(d, h), :] = first[d][128:192, :]
        cov[rows(d, 1 - h), :] = cov_got[d - 1] if d else own_got[128:192, :]
    for d in range(X):
        for k in range(8):
            for n in range(4):
                at = d * 128 + k * 16
                panel[at : at + 16, n * 128 : n * 128 + 128] = panels[d][k * 4 + n]
    for d in range(X):
        product = jnp.dot(
            panel[d * 128 : (d + 1) * 128, :], cov[...], preferred_element_type=F32
        )
        value = carry[d][...].astype(F32) + product * (1.0 / math.sqrt(WIDTH))
        value = value.astype(BF16)
        outs[d][...] = value
        pairs[d // 2][d % 2 * 128 : d % 2 * 128 + 128, :] = value


def innov_kernel(own_got, jac_got, *refs):
    first, sens, sens_got = refs[:X], refs[X : X + 2], refs[X + 2 : X + 4]
    parts, jac, both = refs[-3:]
    h = lax.axis_index("h")
    for d in range(X):
        for side, ref in ((h, first[d]), (1 - h, jac_got.at[d - 1] if d else own_got)):
            to = pl.ds(pl.multiple_of((source(d) * H + side) * 64, 64), 64)
            jac[to, 0:1024] = ref[0:64, :]
            jac[to, 1024:2048] = ref[64:128, :]
    for k in range(2):
        both[k * 256 : (k + 1) * 256, 0:1024] = sens[k][...]
        both[k * 256 : (k + 1) * 256, 1024:2048] = sens_got[k][...]
    value = lax.dot_general(
        jac[...], both[...], (((1,), (1,)), ((), ())), preferred_element_type=F32
    )
    for d in range(X):
        parts[source(d)] = value[:, d * 128 : (d + 1) * 128].astype(BF16)


def final_kernel(got, out):
    total = got[0].astype(F32)
    for k in range(1, X * L * Z):
        total += got[k].astype(F32)
    out[...] = total * (1.0 / math.sqrt(PARAMS))


def assemble_kernel(*refs):
    pieces, out, sems = refs[:X], refs[X], refs[X + 1]
    copies = []
    for d in range(X):
        at = lax.rem(lax.axis_index("x") + d, X)
        copies.append((pieces[d], out.at[:, pl.ds(pl.multiple_of(at * 1024, 1024), 1024)]))
    run_copies(copies, sems)


def ring(d):
    return [(x, (x + d) % X) for x in range(X)]


def over(value, axes):
    return lax.all_to_all(value, axes, split_axis=0, concat_axis=0, tiled=True)


def dma(n):
    return [pltpu.SemaphoreType.DMA((n,))]


def join(first, first_row, rows, behind):
    return call(
        functools.partial(join_kernel, first_row, rows),
        shape(X - 1, rows, 1024),
        first[1:],
        ANY,
        dma(X - 1),
        nbytes=2 * MIB,
        behind=behind,
    )

def body(jacobian, cov_rows, sens_carry):
    give, panel, *packed = call(
        give_kernel,
        [shape(64, 4096), shape(32, 16, 128)] + [shape(192, 1024)] * X,
        (jacobian, cov_rows),
        ANY,
        dma(34 + 3 * X),
        nbytes=4 * MIB,
    )
    got = lax.ppermute(give, "c", SWAP)
    mine = over(panel, ("l", "z", "c"))[0]
    panel = over(jnp.broadcast_to(mine, (32, 16, 128)), ("l", "z", "c"))
    packed = call(
        fill_kernel,
        [shape(192, 1024)] * X,
        (got, *packed),
        ANY,
        dma(X),
        nbytes=MIB,
        aliases={1 + d: d for d in range(X)},
    )
    own_got = lax.ppermute(packed[0], "h", SWAP)
    first = [packed[0]] + [lax.ppermute(packed[d], "x", ring(d)) for d in range(1, X)]
    panels = [panel] + [lax.ppermute(panel, "x", ring(d)) for d in range(1, X)]
    packed = call(
        carry_kernel, [shape(128, 1024)] * X, (sens_carry,), ANY, dma(X), nbytes=2 * MIB
    )
    carry = [packed[0]] + [lax.ppermute(packed[d], "x", ring(d)) for d in range(1, X)]
    cov_rest = join(first, 128, 64, (panel,))
    jac_rest = join(first, 0, 128, (cov_rest, own_got))
    cov_got = lax.ppermute(cov_rest, "h", SWAP)
    jac_got = lax.ppermute(jac_rest, "h", SWAP)
    *sens, low, high = call(
        sens_kernel,
        [shape(128, 1024)] * X + [shape(256, 1024)] * 2,
        (*first, *carry, *panels, own_got, cov_got),
        VMEM,
        [pltpu.VMEM((512, 1024), BF16), pltpu.VMEM((512, WIDTH), BF16)],
        flops=2 * 512 * 512 * 1024,
        nbytes=2 * MIB,
        vmem=12,
    )
    sens_back = [sens[0]] + [lax.ppermute(sens[d], "x", ring(-d)) for d in range(1, X)]
    sens_got = [lax.ppermute(pair, "c", SWAP) for pair in (low, high)]
    parts = call(
        innov_kernel,
        shape(X, 512, 128),
        (own_got, jac_got, *first, low, high, *sens_got),
        VMEM,
        [pltpu.VMEM((512, 2048), BF16)] * 2,
        flops=2 * 512 * 512 * 2048,
        nbytes=2 * MIB,
        vmem=16,
        behind=(sens_back[1], sens_back[3]),
    )
    shared = over(parts.reshape(X * L * Z, 32, 128), ("x", "l", "z"))
    innovation = call(final_kernel, shape(32, 128, kind=F32), (shared,), VMEM, nbytes=2**19, vmem=4)
    sensitivity = call(
        assemble_kernel, shape(128, 4096), sens_back, ANY, dma(X), nbytes=2 * MIB
    )
    return (sensitivity, innovation.T)


def solution(mesh):
    fine = Mesh(mesh.devices.reshape(X, H, L, Z, C), AXES)
    spec = P(("x", "h"), ("l", "z", "c"))
    return jax.shard_map(
        body, mesh=fine, in_specs=(spec,) * 3, out_specs=(spec,) * 2, check_vma=False
    )
```
